512 devices in a mesh: segment: 2 (over core), mp: 64 (over y, z), dp: 4 (over x).
Axes of the slice: x: 4, y: 8, z: 8, core: 2. Of those that a mesh axis runs over, the one named last changes fastest.
Arguments:
- key_value: bfloat16 [8, 128, 96, 2048], P('dp', ('segment', 'mp')), may hold values from -5 to 5
- key_gain: float32 [128], replicated, may hold values from 0.1 to 1.9
- queries: bfloat16 [8, 32, 32, 8192], P('dp', 'segment', None, 'mp'), may hold values from -36 to 36
- tile_count: int32 [8, 32, 32], P('dp', 'segment'), may hold values from 0 to 4
- attn_gate: float32 [1], replicated, may hold values from 0.3 to 1.2
- cotangent: bfloat16 [8, 32, 32, 8192], P('dp', 'segment', None, 'mp'), may hold values from -6 to 6
Outputs:
- attended: bfloat16 [8, 32, 32, 8192], P('dp', 'segment', None, 'mp')
- d_key_value: bfloat16 [8, 128, 96, 2048], P('dp', ('segment', 'mp'))
- d_gain: float32 [128], replicated
- d_gate: float32 [1], replicated
The draws below stay inside these ranges and needn't reach their ends.
Inputs may be any that keep to these rules, and one draw needn't show every extreme that they name: A text token sees the first tile_count tiles of its own sample's image; 0 means it sees none and its output is zero.
All inputs are finite; a program needn't handle non-finite values.
Results may differ from the reference program's by a relative error of at most 0.0034.
The reference program's roundings to bfloat16 on the way count: a program that leaves them out, or rounds other values in their place, can miss the bound.
Values may be sent and summed in bfloat16 or wider, within the bound.
A program may use at most 64 MiB of HBM per device.

```python
import jax
import jax.numpy as jnp
from jax import lax

HEADS = 64
KV_HEADS = 8
HEAD = 128
TILES = 4
PATCH = 96
TXT_S = 32
TILES_ALL = 128
SAMPLES = 32
BATCHES = 8


def draw_key_value(key, part):
    shape = (BATCHES, SAMPLES, TILES, PATCH, KV_HEADS, 2, HEAD)
    fresh = jax.random.fold_in(key, 11)
    result = jnp.clip(jax.random.normal(fresh, shape, jnp.float32), -5.0, 5.0)
    return result.reshape(BATCHES, TILES_ALL, PATCH, KV_HEADS * 2 * HEAD).astype(jnp.bfloat16)


def draw_queries(key, part):
    shape = (BATCHES, SAMPLES, TXT_S, KV_HEADS, HEADS // KV_HEADS, HEAD)
    fresh = jax.random.fold_in(key, 13)
    result = jnp.clip(jax.random.normal(fresh, shape, jnp.float32), -6.0, 6.0)
    return result.reshape(BATCHES, SAMPLES, TXT_S, HEADS * HEAD).astype(jnp.bfloat16)


def plant(values, stream_key, least, largest):
    index_at = [jax.random.randint(jax.random.fold_in(stream_key, axis), (), 0, length) for axis, length in enumerate(values.shape)]
    widest = values.shape.index(max(values.shape))
    next_to = index_at[:widest] + [(index_at[widest] + 1) % values.shape[widest]] + index_at[widest + 1:]
    return values.at[tuple(index_at)].set(least).at[tuple(next_to)].set(largest)


def block_scale(key, shape, pieces, low, largest):
    loudness = 1.0
    for dim, shards_of in pieces:
        heights = jax.random.uniform(jax.random.fold_in(jax.random.fold_in(key, 6), dim), (shards_of,), jnp.float32, low / len(pieces), largest / len(pieces))
        loudness = loudness * jnp.repeat(jnp.exp(heights), shape[dim] // shards_of).reshape((-1,) + (1,) * (len(shape) - 1 - dim))
    return loudness


def centred(key, shape, spread, reach, pieces=(), kind=jnp.bfloat16):
    entries = jax.random.normal(key, shape, jnp.float32) * spread
    if len(pieces) > 0:
        entries = block_scale(key, shape, pieces, -0.22, 0.18) * entries
    return jnp.clip(entries, min=-reach, max=reach).astype(kind)


def setup_inputs(seed: int = 0) -> dict:
    splits = jax.random.split(jax.random.key(seed), 7)
    key_value = draw_key_value(jax.random.fold_in(splits[6], 71), 0)
    key_gain = jnp.clip(1.0 + 0.18 * jax.random.normal(splits[1], (HEAD,), jnp.float32), 0.1, 1.9)
    queries = draw_queries(jax.random.fold_in(splits[6], 71), 0)
    tile_count = plant(jax.random.randint(splits[3], (BATCHES, SAMPLES, TXT_S), 0, TILES + 1), jax.random.fold_in(splits[3], 1), 0, TILES).astype(jnp.int32)
    attn_gate = jnp.clip(jax.random.uniform(splits[4], (1,), jnp.float32, 0.3, 1.2), 0.3, 1.2)
    cotangent = centred(splits[5], (BATCHES, SAMPLES, TXT_S, HEADS * HEAD), 1.0, 6.0, ((0, 4), (1, 2), (3, 64)))
    return {"key_value": key_value, "key_gain": key_gain, "queries": queries, "tile_count": tile_count, "attn_gate": attn_gate, "cotangent": cotangent}


def to_low(values):
    return lax.optimization_barrier(values.astype(jnp.bfloat16)).astype(jnp.float32)

def reference(key_value, key_gain, queries, tile_count, attn_gate, cotangent):
    group = HEADS // KV_HEADS
    keys_all = TILES * PATCH
    scale = 1.0 / HEAD ** 0.5
    gate = jnp.tanh(attn_gate[0])
    key_tile = jnp.arange(keys_all, dtype=jnp.int32) // PATCH

    def one_batch(items):
        state_rows, query_rows, counts, cotan = items
        parts = state_rows.reshape(SAMPLES, keys_all, KV_HEADS, 2, HEAD).astype(jnp.float32)
        raw_keys = parts[:, :, :, 0]
        values = parts[:, :, :, 1]
        inverse = lax.rsqrt(lax.optimization_barrier(jnp.mean(raw_keys * raw_keys, axis=-1, keepdims=True)) + 1e-05)
        unit_key = raw_keys * inverse
        keys = to_low(unit_key * key_gain)
        query_heads = query_rows.reshape(SAMPLES, TXT_S, KV_HEADS, group, HEAD).astype(jnp.float32)
        logits = jnp.einsum('stkgd,snkd->skgtn', query_heads, keys) * scale
        allowed = key_tile[None, None, :] < jnp.maximum(counts, 1)[:, :, None]
        logits = jnp.where(allowed[:, None, None], logits, -1e+30)
        top = lax.optimization_barrier(jnp.max(logits, axis=-1, keepdims=True))
        exps = jnp.exp(logits - top)
        probs = exps / lax.optimization_barrier(jnp.sum(exps, axis=-1, keepdims=True))
        probs_low = to_low(probs)
        mixed = jnp.einsum('skgtn,snkd->stkgd', probs_low, values)
        live = (counts > 0).astype(jnp.float32)[:, :, None, None, None]
        attended = (gate * live * mixed).astype(jnp.bfloat16).reshape(SAMPLES, TXT_S, HEADS * HEAD)
        cotan_heads = cotan.reshape(SAMPLES, TXT_S, KV_HEADS, group, HEAD).astype(jnp.float32)
        gate_part = jnp.sum(cotan_heads * live * mixed)
        d_mixed = to_low(gate * live * cotan_heads)
        d_probs = jnp.einsum('stkgd,snkd->skgtn', d_mixed, values)
        inner = lax.optimization_barrier(jnp.sum(probs * d_probs, axis=-1, keepdims=True))
        d_logits = to_low(probs * (d_probs - inner) * scale)
        d_keys = to_low(jnp.einsum('skgtn,stkgd->snkgd', d_logits, query_heads))
        d_values = to_low(jnp.einsum('skgtn,stkgd->snkgd', probs_low, d_mixed))
        key_part = to_low(lax.optimization_barrier(jnp.sum(d_keys, axis=3)))
        value_part = to_low(lax.optimization_barrier(jnp.sum(d_values, axis=3)))
        gain_part = lax.optimization_barrier(jnp.sum(key_part * unit_key, axis=(0, 1, 2)))
        scaled = key_part * key_gain
        d_unit = inverse * (scaled - unit_key * lax.optimization_barrier(jnp.mean(scaled * unit_key, axis=-1, keepdims=True)))
        d_rows = jnp.stack([d_unit, value_part], axis=3).astype(jnp.bfloat16)
        d_rows = d_rows.reshape(TILES_ALL, PATCH, KV_HEADS * 2 * HEAD)
        return (attended, d_rows, gain_part, gate_part)
    attended, d_key_value, gains, gates = lax.map(one_batch, (key_value, queries, tile_count, cotangent))
    d_gain = lax.optimization_barrier(jnp.sum(gains, axis=0))
    d_gate = (jnp.sum(gates) * (1.0 - gate * gate)).reshape(1)
    return (attended, d_key_value, d_gain, d_gate)
```

```python
import jax
import jax.numpy as jnp
from jax import lax
from jax.experimental import pallas as pl
from jax.experimental.pallas import tpu as pltpu
from jax.sharding import PartitionSpec as P

HEAD = 128
TILES = 4
PATCH = 96
KEYS = TILES * PATCH
MICRO = 2
SAMPLES = 16
TEXT = 32
GROUP = 8
OWN_KV = 2
OWN_HEADS = OWN_KV * GROUP
ROWS = GROUP * TEXT
WIDE = 2 * HEAD
SCALE = 1.0 / HEAD**0.5


def dot(a, b, dims):
    return lax.dot_general(a, b, (dims, ((), ())), preferred_element_type=jnp.float32)


def kernel(
    kv_ref, gain_ref, q_ref, count_ref, gate_ref, cot_ref,
    att_ref, dkv_ref, dgain_ref, dgate_ref,
    kvbuf, qbuf, cbuf, gbuf, abuf, qblk, dblk, red_src, red1, red2, red3,
    kv_send, kv_recv, q_send, q_recv, c_send, c_recv, g_send, g_recv, a_send, a_recv,
    r1_send, r1_recv, r2_send, r2_recv, r3_send, r3_recv,
):
    me = lax.axis_index("mp")
    seg = lax.axis_index("segment")
    dp = lax.axis_index("dp")
    n_dp = lax.axis_size("dp")
    n_rep = n_dp * lax.axis_size("segment")
    sample = me // TILES
    place = me % TILES
    part = (place + TILES - (sample // 2) % TILES) % TILES
    my_part = me // OWN_HEADS
    my_slot = me % OWN_HEADS
    my_unit = my_slot // GROUP
    rep = dp * lax.axis_size("segment") + seg

    def worker(n):
        return n * TILES + (my_part + n // 2) % TILES

    def owner(i):
        return part * OWN_HEADS + i

    def member(i):
        return sample * TILES + i

    def member_part(i):
        return (i + TILES - (sample // 2) % TILES) % TILES

    def rep_id(i):
        return {"segment": i % lax.axis_size("segment"), "dp": i // lax.axis_size("segment")}

    barrier = pltpu.get_barrier_semaphore()
    has_self = (part == my_part).astype(jnp.int32)

    def greet_heads(i, _):
        @pl.when(worker(i) != me)
        def _():
            pl.semaphore_signal(barrier, inc=1, device_id={"mp": worker(i)})

        @pl.when(owner(i) != me)
        def _():
            pl.semaphore_signal(barrier, inc=1, device_id={"mp": owner(i)})
        return 0

    def greet_members(i, _):
        @pl.when(i != place)
        def _():
            pl.semaphore_signal(barrier, inc=1, device_id={"mp": member(i)})
        return 0

    def greet_reps(i, _):
        @pl.when(i != rep)
        def _():
            pl.semaphore_signal(barrier, inc=1, device_id=rep_id(i))
        return 0

    lax.fori_loop(0, TILES, greet_members, 0)
    lax.fori_loop(0, SAMPLES, greet_heads, 0)
    lax.fori_loop(0, n_rep, greet_reps, 0)
    qblk[...] = jnp.zeros_like(qblk)
    dblk[...] = jnp.zeros_like(dblk)
    pl.semaphore_wait(barrier, 2 * (SAMPLES - has_self) + TILES - 1 + n_rep - 1)

    def columns(p, u):
        return pl.ds(pl.multiple_of((p * OWN_KV + u) * WIDE, WIDE), WIDE)

    def kv_copy(b, u, i):
        return pltpu.make_async_remote_copy(
            kv_ref.at[b, 0, :, columns(member_part(i), u)], kvbuf.at[b, u, place],
            kv_send.at[b, u, i], kv_recv.at[b, u], device_id={"mp": member(i)},
        )

    def q_copy(b, n):
        return pltpu.make_async_remote_copy(
            q_ref.at[b, n], qbuf.at[b, my_slot], q_send.at[b, n], q_recv.at[b, my_unit],
            device_id={"mp": worker(n)},
        )

    def c_copy(b, n):
        return pltpu.make_async_remote_copy(
            cot_ref.at[b, n], cbuf.at[b, my_slot], c_send.at[b, n], c_recv.at[b, my_unit],
            device_id={"mp": worker(n)},
        )

    def send_kv(b, u):
        def step(i, _):
            @pl.when(i != place)
            def _():
                kv_copy(b, u, i).start()
            return 0
        lax.fori_loop(0, TILES, step, 0)
        pltpu.make_async_copy(
            kv_ref.at[b, 0, :, columns(part, u)], kvbuf.at[b, u, place], kv_recv.at[b, u]
        ).start()

    def send_heads(b):
        def q_step(n, _):
            @pl.when(worker(n) != me)
            def _():
                q_copy(b, n).start()

            @pl.when(worker(n) == me)
            def _():
                pltpu.make_async_copy(q_ref.at[b, n], qbuf.at[b, my_slot], q_recv.at[b, my_unit]).start()
            return 0

        def c_step(n, _):
            @pl.when(worker(n) != me)
            def _():
                c_copy(b, n).start()

            @pl.when(worker(n) == me)
            def _():
                pltpu.make_async_copy(cot_ref.at[b, n], cbuf.at[b, my_slot], c_recv.at[b, my_unit]).start()
            return 0

        lax.fori_loop(0, SAMPLES, q_step, 0)
        lax.fori_loop(0, SAMPLES, c_step, 0)

    for b in range(MICRO):
        send_kv(b, 0)
        send_heads(b)
        send_kv(b, 1)

    gate = jnp.tanh(jnp.full((1, HEAD), gate_ref[0], jnp.float32))
    gain = gain_ref[...]
    token_of = (lax.broadcasted_iota(jnp.int32, (ROWS, TEXT), 0) & (TEXT - 1)) == (
        lax.broadcasted_iota(jnp.int32, (ROWS, TEXT), 1)
    )
    spread = token_of.astype(jnp.bfloat16)
    key_row = lax.broadcasted_iota(jnp.int32, (KEYS, ROWS), 0)

    def g_copy(b, u, i):
        return pltpu.make_async_remote_copy(
            gbuf.at[b, u, i], dkv_ref.at[b, 0, :, columns(part, u)], g_send.at[b, u, i], g_recv.at[0],
            device_id={"mp": member(i)},
        )

    def a_copy(b, i):
        return pltpu.make_async_remote_copy(
            abuf.at[b, i], att_ref.at[b, sample], a_send.at[b, i], a_recv.at[0],
            device_id={"mp": owner(i)},
        )

    def unit(step, carry):
        gain_sum, gate_sum = carry
        b = step // OWN_KV
        u = step % OWN_KV
        heads = pl.ds(u * GROUP, GROUP)
        q_view, c_view = qbuf.at[b, heads], cbuf.at[b, heads]
        counts = count_ref[b, pl.ds(sample, 1), :].astype(jnp.float32).astype(jnp.bfloat16)
        count_col = dot(spread, jnp.broadcast_to(counts, (HEAD, TEXT)), ((1,), (1,)))
        count_row = dot(jnp.broadcast_to(counts, (8, TEXT)), spread, ((1,), (1,)))[0:1]
        live = (count_col > 0.5).astype(jnp.float32)
        gate_live = gate * live
        limit = (jnp.maximum(count_row, 1.0) * PATCH).astype(jnp.int32)

        pltpu.make_async_copy(kvbuf.at[b, u], kvbuf.at[b, u], kv_recv.at[b, u]).wait()
        kv = kvbuf[b, u].reshape(KEYS, WIDE)
        raw = kv[:, :HEAD].astype(jnp.float32)
        values = kv[:, HEAD:]
        inverse = lax.rsqrt(jnp.mean(raw * raw, axis=-1, keepdims=True) + 1e-05)
        unit_key = raw * inverse
        keys = (unit_key * gain).astype(jnp.bfloat16)

        pltpu.make_async_copy(q_view, q_view, q_recv.at[b, u]).wait()
        queries = q_view[...].reshape(ROWS, HEAD)
        logits = dot(keys, queries, ((1,), (1,))) * SCALE
        logits = jnp.where(key_row < limit, logits, -1e30)
        exps = jnp.exp(logits - jnp.max(logits, axis=0, keepdims=True))
        probs = exps / jnp.sum(exps, axis=0, keepdims=True)
        probs_low = probs.astype(jnp.bfloat16)
        mixed = dot(probs_low, values, ((0,), (0,)))
        abuf[b, heads] = (gate_live * mixed).astype(jnp.bfloat16).reshape(GROUP, TEXT, HEAD)

        def a_step(k, _):
            i = u * GROUP + k

            @pl.when(owner(i) != me)
            def _():
                a_copy(b, i).start()

            @pl.when(owner(i) == me)
            def _():
                pltpu.make_async_copy(abuf.at[b, i], att_ref.at[b, sample], a_recv.at[0]).start()
            return 0

        lax.fori_loop(0, GROUP, a_step, 0)

        pltpu.make_async_copy(c_view, c_view, c_recv.at[b, u]).wait()
        cotan = c_view[...].reshape(ROWS, HEAD).astype(jnp.float32)
        gate_sum = gate_sum + jnp.sum(cotan * live * mixed, axis=0, keepdims=True)
        d_mixed = (gate_live * cotan).astype(jnp.bfloat16)
        d_probs = dot(values, d_mixed, ((1,), (1,)))
        inner = jnp.sum(probs * d_probs, axis=0, keepdims=True)
        d_logits = (probs * (d_probs - inner) * SCALE).astype(jnp.bfloat16)
        for h in range(GROUP):
            rows, cols = slice(h * TEXT, (h + 1) * TEXT), slice(h * HEAD, (h + 1) * HEAD)
            qblk[rows, cols] = queries[rows]
            dblk[rows, cols] = d_mixed[rows]

        def head_sum(left, blocks):
            total = jnp.zeros((KEYS, HEAD), jnp.float32)
            for h in range(0, GROUP, 2):
                pair = dot(left, blocks[:, h * HEAD:(h + 2) * HEAD], ((1,), (0,)))
                pair = pair.astype(jnp.bfloat16).astype(jnp.float32)
                total = total + pair[:, :HEAD] + pair[:, HEAD:]
            return total.astype(jnp.bfloat16)

        key_part = head_sum(d_logits, qblk).astype(jnp.float32)
        value_part = head_sum(probs_low, dblk)
        gain_sum = gain_sum + jnp.sum(key_part * unit_key, axis=0, keepdims=True)
        scaled = key_part * gain
        d_key = inverse * (scaled - unit_key * jnp.mean(scaled * unit_key, axis=-1, keepdims=True))
        gbuf[b, u, :, :, :HEAD] = d_key.astype(jnp.bfloat16).reshape(TILES, PATCH, HEAD)
        gbuf[b, u, :, :, HEAD:] = value_part.reshape(TILES, PATCH, HEAD)

        def g_step(i, _):
            @pl.when(i != place)
            def _():
                g_copy(b, u, i).start()
            return 0

        lax.fori_loop(0, TILES, g_step, 0)
        pltpu.make_async_copy(
            gbuf.at[b, u, place], dkv_ref.at[b, 0, :, columns(part, u)], g_recv.at[0]
        ).start()
        return gain_sum, gate_sum

    zero = jnp.zeros((1, HEAD), jnp.float32)
    gain_sum, gate_sum = lax.fori_loop(0, MICRO * OWN_KV, unit, (zero, zero))

    row = lax.broadcasted_iota(jnp.int32, (8, HEAD), 0)

    def spread_sums(gain_sum, gate_sum):
        return jnp.where(row == 0, gain_sum, jnp.where(row == 1, gate_sum, 0.0))

    red_src[0] = spread_sums(gain_sum, gate_sum)

    def r1_copy(n):
        return pltpu.make_async_remote_copy(
            red_src.at[0], red1.at[my_slot], r1_send.at[n], r1_recv.at[0], device_id={"mp": worker(n)}
        )

    def r1_step(n, _):
        @pl.when(worker(n) != me)
        def _():
            r1_copy(n).start()

        @pl.when(worker(n) == me)
        def _():
            pltpu.make_async_copy(red_src.at[0], red1.at[my_slot], r1_recv.at[0]).start()
        return 0

    lax.fori_loop(0, SAMPLES, r1_step, 0)
    pltpu.make_async_copy(red1, red1, r1_recv.at[0]).wait()
    red_src[1] = jnp.sum(red1[...], axis=0)

    def r2_copy(i):
        return pltpu.make_async_remote_copy(
            red_src.at[1], red2.at[place], r2_send.at[i], r2_recv.at[0], device_id={"mp": member(i)}
        )

    def r2_step(i, _):
        @pl.when(i != place)
        def _():
            r2_copy(i).start()
        return 0

    lax.fori_loop(0, TILES, r2_step, 0)
    pltpu.make_async_copy(red_src.at[1], red2.at[place], r2_recv.at[0]).start()
    pltpu.make_async_copy(red2, red2, r2_recv.at[0]).wait()
    red_src[2] = jnp.sum(red2[...], axis=0)

    def r3_copy(i):
        return pltpu.make_async_remote_copy(
            red_src.at[2], red3.at[rep], r3_send.at[i], r3_recv.at[0], device_id=rep_id(i)
        )

    def r3_step(i, _):
        @pl.when(i != rep)
        def _():
            r3_copy(i).start()
        return 0

    lax.fori_loop(0, n_rep, r3_step, 0)
    pltpu.make_async_copy(red_src.at[2], red3.at[rep], r3_recv.at[0]).start()

    def heads_sent(n, _):
        @pl.when(worker(n) != me)
        def _():
            for b in range(MICRO):
                q_copy(b, n).wait_send()
                c_copy(b, n).wait_send()
            r1_copy(n).wait_send()

        @pl.when(owner(n) != me)
        def _():
            for b in range(MICRO):
                a_copy(b, n).wait_send()
        return 0

    def members_sent(i, _):
        @pl.when(i != place)
        def _():
            for b in range(MICRO):
                for u in range(OWN_KV):
                    kv_copy(b, u, i).wait_send()
                    g_copy(b, u, i).wait_send()
            r2_copy(i).wait_send()
        return 0

    def reps_sent(i, _):
        @pl.when(i != rep)
        def _():
            r3_copy(i).wait_send()
        return 0

    lax.fori_loop(0, SAMPLES, heads_sent, 0)
    lax.fori_loop(0, TILES, members_sent, 0)
    lax.fori_loop(0, n_rep, reps_sent, 0)

    pltpu.make_async_copy(red3, red3, r3_recv.at[0]).wait()
    total = jnp.sum(red3[...], axis=0)
    dgain_ref[...] = total[0:1]
    dgate_ref[...] = jnp.sum(total[1:2], axis=1, keepdims=True) * (1.0 - gate * gate)

    pltpu.make_async_copy(att_ref, att_ref, a_recv.at[0]).wait()
    pltpu.make_async_copy(dkv_ref, dkv_ref, g_recv.at[0]).wait()


def shards(key_value, key_gain, queries, tile_count, attn_gate, cotangent):
    n_rep = lax.axis_size("dp") * lax.axis_size("segment")
    vmem, anywhere = pl.BlockSpec(memory_space=pltpu.VMEM), pl.BlockSpec(memory_space=pl.ANY)
    dma = pltpu.SemaphoreType.DMA
    bf16, f32 = jnp.bfloat16, jnp.float32
    attended, d_key_value, d_gain, d_gate = pl.pallas_call(
        kernel,
        out_shape=(
            jax.ShapeDtypeStruct(queries.shape, bf16),
            jax.ShapeDtypeStruct(key_value.shape, bf16),
            jax.ShapeDtypeStruct((1, HEAD), f32),
            jax.ShapeDtypeStruct((1, HEAD), f32),
        ),
        in_specs=[anywhere, vmem, anywhere, vmem, pl.BlockSpec(memory_space=pltpu.SMEM), anywhere],
        out_specs=(anywhere, anywhere, vmem, vmem),
        scratch_shapes=[
            pltpu.VMEM((MICRO, OWN_KV, TILES, PATCH, WIDE), bf16),
            pltpu.VMEM((MICRO, OWN_HEADS, TEXT, HEAD), bf16),
            pltpu.VMEM((MICRO, OWN_HEADS, TEXT, HEAD), bf16),
            pltpu.VMEM((MICRO, OWN_KV, TILES, PATCH, WIDE), bf16),
            pltpu.VMEM((MICRO, OWN_HEADS, TEXT, HEAD), bf16),
            pltpu.VMEM((ROWS, GROUP * HEAD), bf16),
            pltpu.VMEM((ROWS, GROUP * HEAD), bf16),
            pltpu.VMEM((3, 8, HEAD), f32),
            pltpu.VMEM((SAMPLES, 8, HEAD), f32),
            pltpu.VMEM((TILES, 8, HEAD), f32),
            pltpu.VMEM((n_rep, 8, HEAD), f32),
            dma((MICRO, OWN_KV, TILES)), dma((MICRO, OWN_KV)),
            dma((MICRO, SAMPLES)), dma((MICRO, OWN_KV)),
            dma((MICRO, SAMPLES)), dma((MICRO, OWN_KV)),
            dma((MICRO, OWN_KV, TILES)), dma((1,)),
            dma((MICRO, OWN_HEADS)), dma((1,)),
            dma((SAMPLES,)), dma((1,)), dma((TILES,)), dma((1,)), dma((n_rep,)), dma((1,)),
        ],
        compiler_params=pltpu.CompilerParams(
            collective_id=0, has_side_effects=True, vmem_limit_bytes=48 * 1024 * 1024
        ),
        name="cross_attention",
    )(key_value, key_gain.reshape(1, HEAD), queries, tile_count, attn_gate, cotangent)
    return attended, d_key_value, d_gain.reshape(HEAD), d_gate[0, :1]


def solution(mesh):
    in_specs = (
        P("dp", ("segment", "mp"), None, None),
        P(),
        P("dp", "segment", None, "mp"),
        P("dp", "segment", None),
        P(),
        P("dp", "segment", None, "mp"),
    )
    out_specs = (P("dp", "segment", None, "mp"), P("dp", ("segment", "mp"), None, None), P(), P())
    return jax.shard_map(shards, mesh=mesh, in_specs=in_specs, out_specs=out_specs, check_vma=False)
```

```python
import jax
import jax.numpy as jnp
from jax import lax
from jax.experimental import pallas as pl
from jax.experimental.pallas import tpu as pltpu
from jax.sharding import PartitionSpec as P

HEAD = 128
TILES = 4
PATCH = 96
KEYS = TILES * PATCH
MICRO = 2
SAMPLES = 16
TEXT = 32
GROUP = 8
OWN_KV = 2
OWN_HEADS = OWN_KV * GROUP
ROWS = GROUP * TEXT
WIDE = 2 * HEAD
GRADS_AT_ONCE = 1
GRADS_AFTER = ((1,), (2,), (3,))
SCALE = 1.0 / HEAD**0.5


def dot(a, b, dims):
    return lax.dot_general(a, b, (dims, ((), ())), preferred_element_type=jnp.float32)


def kernel(
    kv_ref, gain_ref, q_ref, count_ref, gate_ref, cot_ref,
    att_ref, dkv_ref, dgain_ref, dgate_ref,
    kvbuf, qbuf, cbuf, gbuf, abuf, qblk, dblk, red_src, red1, red2, red3,
    kv_send, kv_recv, q_send, q_recv, c_send, c_recv, g_send, g_recv, a_send, a_recv,
    r1_send, r1_recv, r2_send, r2_recv, r3_send, r3_recv,
    gain_v, count_v, small_sem,
):
    me = lax.axis_index("mp")
    seg = lax.axis_index("segment")
    dp = lax.axis_index("dp")
    n_dp = lax.axis_size("dp")
    n_rep = n_dp * lax.axis_size("segment")
    sample = me // TILES
    place = me % TILES
    part = (place + TILES - (sample // 2) % TILES) % TILES
    my_part = me // OWN_HEADS
    my_slot = me % OWN_HEADS
    my_unit = my_slot // GROUP
    rep = dp * lax.axis_size("segment") + seg

    def worker(n):
        return n * TILES + (my_part + n // 2) % TILES

    def owner(i):
        return part * OWN_HEADS + i

    def member(i):
        return sample * TILES + i

    def member_part(i):
        return (i + TILES - (sample // 2) % TILES) % TILES

    def turn(k):
        r = k // 2
        row = sample // 2 + 8 + ((r + 1) // 2) * (1 - 2 * (r % 2))
        return (row % 8) * 2 + (k + sample) % 2

    def other(k):
        return (place + 1 + k) % TILES

    def rep_id(i):
        return {"segment": i % lax.axis_size("segment"), "dp": i // lax.axis_size("segment")}

    smalls = [
        pltpu.make_async_copy(gain_ref, gain_v, small_sem.at[0]),
        pltpu.make_async_copy(count_ref, count_v, small_sem.at[1]),
    ]
    for copy in smalls:
        copy.start()

    barrier = pltpu.get_barrier_semaphore()
    has_self = (part == my_part).astype(jnp.int32)

    def greet_heads(i, _):
        @pl.when(worker(i) != me)
        def _():
            pl.semaphore_signal(barrier, inc=1, device_id={"mp": worker(i)})

        @pl.when(owner(i) != me)
        def _():
            pl.semaphore_signal(barrier, inc=1, device_id={"mp": owner(i)})
        return 0

    def greet_members(i, _):
        @pl.when(i != place)
        def _():
            pl.semaphore_signal(barrier, inc=1, device_id={"mp": member(i)})
        return 0

    def greet_reps(i, _):
        @pl.when(i != rep)
        def _():
            pl.semaphore_signal(barrier, inc=1, device_id=rep_id(i))
        return 0

    lax.fori_loop(0, TILES, greet_members, 0)
    lax.fori_loop(0, SAMPLES, greet_heads, 0)
    lax.fori_loop(0, n_rep, greet_reps, 0)
    qblk[...] = jnp.zeros_like(qblk)
    dblk[...] = jnp.zeros_like(dblk)
    pl.semaphore_wait(barrier, 2 * (SAMPLES - has_self) + TILES - 1 + n_rep - 1)

    def columns(p, u):
        return pl.ds(pl.multiple_of((p * OWN_KV + u) * WIDE, WIDE), WIDE)

    def kv_copy(b, u, i):
        return pltpu.make_async_remote_copy(
            kv_ref.at[b, 0, :, columns(member_part(i), u)], kvbuf.at[b, u, place],
            kv_send.at[b, u, i], kv_recv.at[b, u], device_id={"mp": member(i)},
        )

    def q_copy(b, n):
        return pltpu.make_async_remote_copy(
            q_ref.at[b, n], qbuf.at[b, my_slot], q_send.at[b, n], q_recv.at[b, my_unit],
            device_id={"mp": worker(n)},
        )

    def c_copy(b, n):
        return pltpu.make_async_remote_copy(
            cot_ref.at[b, n], cbuf.at[b, my_slot], c_send.at[b, n], c_recv.at[b, my_unit],
            device_id={"mp": worker(n)},
        )

    def send_kv(b, u):
        def step(k, _):
            kv_copy(b, u, other(k)).start()
            return 0
        lax.fori_loop(0, TILES - 1, step, 0)
        pltpu.make_async_copy(
            kv_ref.at[b, 0, :, columns(part, u)], kvbuf.at[b, u, place], kv_recv.at[b, u]
        ).start()

    def send_heads(b):
        def q_step(k, _):
            n = turn(k)

            @pl.when(worker(n) != me)
            def _():
                q_copy(b, n).start()

            @pl.when(worker(n) == me)
            def _():
                pltpu.make_async_copy(q_ref.at[b, n], qbuf.at[b, my_slot], q_recv.at[b, my_unit]).start()
            return 0

        def c_step(k, _):
            n = turn(k)

            @pl.when(worker(n) != me)
            def _():
                c_copy(b, n).start()

            @pl.when(worker(n) == me)
            def _():
                pltpu.make_async_copy(cot_ref.at[b, n], cbuf.at[b, my_slot], c_recv.at[b, my_unit]).start()
            return 0

        lax.fori_loop(0, SAMPLES, q_step, 0)
        lax.fori_loop(0, SAMPLES, c_step, 0)

    for b in range(MICRO):
        send_kv(b, 0)
        send_heads(b)
        send_kv(b, 1)

    for copy in smalls:
        copy.wait()
    gate = jnp.tanh(jnp.full((1, HEAD), gate_ref[0], jnp.float32))
    gain = gain_v[...]
    token_of = (lax.broadcasted_iota(jnp.int32, (ROWS, TEXT), 0) & (TEXT - 1)) == (
        lax.broadcasted_iota(jnp.int32, (ROWS, TEXT), 1)
    )
    spread = token_of.astype(jnp.bfloat16)
    key_row = lax.broadcasted_iota(jnp.int32, (KEYS, ROWS), 0)

    def g_copy(b, u, i):
        return pltpu.make_async_remote_copy(
            gbuf.at[b, u, i], dkv_ref.at[b, 0, :, columns(part, u)], g_send.at[b, u, i], g_recv.at[0],
            device_id={"mp": member(i)},
        )

    def a_copy(b, i):
        return pltpu.make_async_remote_copy(
            abuf.at[b, i], att_ref.at[b, sample], a_send.at[b, i], a_recv.at[0],
            device_id={"mp": owner(i)},
        )

    def send_grads(b, u):
        def g_step(k, _):
            g_copy(b, u, other(k)).start()
            return 0

        lax.fori_loop(0, TILES - 1, g_step, 0)
        pltpu.make_async_copy(
            gbuf.at[b, u, place], dkv_ref.at[b, 0, :, columns(part, u)], g_recv.at[0]
        ).start()

    def send_attended(b, u):
        def a_step(k, _):
            i = u * GROUP + (k + me) % GROUP

            @pl.when(owner(i) != me)
            def _():
                a_copy(b, i).start()

            @pl.when(owner(i) == me)
            def _():
                pltpu.make_async_copy(abuf.at[b, i], att_ref.at[b, sample], a_recv.at[0]).start()
            return 0

        lax.fori_loop(0, GROUP, a_step, 0)

    def unit(step, carry):
        gain_sum, gate_sum = carry
        b = step // OWN_KV
        u = step % OWN_KV
        heads = pl.ds(u * GROUP, GROUP)
        q_view, c_view = qbuf.at[b, heads], cbuf.at[b, heads]
        counts = count_v[b, pl.ds(sample, 1), :].astype(jnp.float32).astype(jnp.bfloat16)
        count_col = dot(spread, jnp.broadcast_to(counts, (HEAD, TEXT)), ((1,), (1,)))
        count_row = dot(jnp.broadcast_to(counts, (8, TEXT)), spread, ((1,), (1,)))[0:1]
        live = (count_col > 0.5).astype(jnp.float32)
        gate_live = gate * live
        limit = (jnp.maximum(count_row, 1.0) * PATCH).astype(jnp.int32)

        pltpu.make_async_copy(kvbuf.at[b, u], kvbuf.at[b, u], kv_recv.at[b, u]).wait()
        kv = kvbuf[b, u].reshape(KEYS, WIDE)
        raw = kv[:, :HEAD].astype(jnp.float32)
        values = kv[:, HEAD:]
        inverse = lax.rsqrt(jnp.mean(raw * raw, axis=-1, keepdims=True) + 1e-05)
        unit_key = raw * inverse
        keys = (unit_key * gain).astype(jnp.bfloat16)

        pltpu.make_async_copy(q_view, q_view, q_recv.at[b, u]).wait()
        queries = q_view[...].reshape(ROWS, HEAD)
        logits = dot(keys, queries, ((1,), (1,))) * SCALE
        logits = jnp.where(key_row < limit, logits, -1e30)
        exps = jnp.exp(logits - jnp.max(logits, axis=0, keepdims=True))
        probs = exps / jnp.sum(exps, axis=0, keepdims=True)
        probs_low = probs.astype(jnp.bfloat16)
        mixed = dot(probs_low, values, ((0,), (0,)))
        abuf[b, heads] = (gate_live * mixed).astype(jnp.bfloat16).reshape(GROUP, TEXT, HEAD)

        send_attended(b, u)

        pltpu.make_async_copy(c_view, c_view, c_recv.at[b, u]).wait()
        cotan = c_view[...].reshape(ROWS, HEAD).astype(jnp.float32)
        gate_sum = gate_sum + jnp.sum(cotan * live * mixed, axis=0, keepdims=True)
        d_mixed = (gate_live * cotan).astype(jnp.bfloat16)
        d_probs = dot(values, d_mixed, ((1,), (1,)))
        inner = jnp.sum(probs * d_probs, axis=0, keepdims=True)
        d_logits = (probs * (d_probs - inner) * SCALE).astype(jnp.bfloat16)
        for h in range(GROUP):
            rows, cols = slice(h * TEXT, (h + 1) * TEXT), slice(h * HEAD, (h + 1) * HEAD)
            qblk[rows, cols] = queries[rows]
            dblk[rows, cols] = d_mixed[rows]

        def head_sum(left, blocks):
            total = jnp.zeros((KEYS, HEAD), jnp.float32)
            for h in range(0, GROUP, 2):
                pair = dot(left, blocks[:, h * HEAD:(h + 2) * HEAD], ((1,), (0,)))
                pair = pair.astype(jnp.bfloat16).astype(jnp.float32)
                total = total + pair[:, :HEAD] + pair[:, HEAD:]
            return total.astype(jnp.bfloat16)

        key_part = head_sum(d_logits, qblk).astype(jnp.float32)
        value_part = head_sum(probs_low, dblk)
        gain_sum = gain_sum + jnp.sum(key_part * unit_key, axis=0, keepdims=True)
        scaled = key_part * gain
        d_key = inverse * (scaled - unit_key * jnp.mean(scaled * unit_key, axis=-1, keepdims=True))
        gbuf[b, u, :, :, :HEAD] = d_key.astype(jnp.bfloat16).reshape(TILES, PATCH, HEAD)
        gbuf[b, u, :, :, HEAD:] = value_part.reshape(TILES, PATCH, HEAD)


        @pl.when(step < GRADS_AT_ONCE)
        def _():
            send_grads(b, u)

        return gain_sum, gate_sum

    zero = jnp.zeros((1, HEAD), jnp.float32)
    gain_sum, gate_sum = lax.fori_loop(0, MICRO * OWN_KV, unit, (zero, zero))

    row = lax.broadcasted_iota(jnp.int32, (8, HEAD), 0)

    def spread_sums(gain_sum, gate_sum):
        return jnp.where(row == 0, gain_sum, jnp.where(row == 1, gate_sum, 0.0))

    red_src[0] = spread_sums(gain_sum, gate_sum)

    def r1_copy(n):
        return pltpu.make_async_remote_copy(
            red_src.at[0], red1.at[my_slot], r1_send.at[n], r1_recv.at[0], device_id={"mp": worker(n)}
        )

    def r1_step(k, _):
        n = turn(k)

        @pl.when(worker(n) != me)
        def _():
            r1_copy(n).start()

        @pl.when(worker(n) == me)
        def _():
            pltpu.make_async_copy(red_src.at[0], red1.at[my_slot], r1_recv.at[0]).start()
        return 0

    lax.fori_loop(0, SAMPLES, r1_step, 0)
    for step in GRADS_AFTER[0]:
        send_grads(step // OWN_KV, step % OWN_KV)
    pltpu.make_async_copy(red1, red1, r1_recv.at[0]).wait()
    red_src[1] = jnp.sum(red1[...], axis=0)

    def r2_copy(i):
        return pltpu.make_async_remote_copy(
            red_src.at[1], red2.at[place], r2_send.at[i], r2_recv.at[0], device_id={"mp": member(i)}
        )

    def r2_step(k, _):
        r2_copy(other(k)).start()
        return 0

    lax.fori_loop(0, TILES - 1, r2_step, 0)
    pltpu.make_async_copy(red_src.at[1], red2.at[place], r2_recv.at[0]).start()
    for step in GRADS_AFTER[1]:
        send_grads(step // OWN_KV, step % OWN_KV)
    pltpu.make_async_copy(red2, red2, r2_recv.at[0]).wait()
    red_src[2] = jnp.sum(red2[...], axis=0)

    def r3_copy(i):
        return pltpu.make_async_remote_copy(
            red_src.at[2], red3.at[rep], r3_send.at[i], r3_recv.at[0], device_id=rep_id(i)
        )

    def r3_step(i, _):
        @pl.when(i != rep)
        def _():
            r3_copy(i).start()
        return 0

    lax.fori_loop(0, n_rep, r3_step, 0)
    pltpu.make_async_copy(red_src.at[2], red3.at[rep], r3_recv.at[0]).start()

    for step in GRADS_AFTER[2]:
        send_grads(step // OWN_KV, step % OWN_KV)

    def heads_sent(n, _):
        @pl.when(worker(n) != me)
        def _():
            for b in range(MICRO):
                q_copy(b, n).wait_send()
                c_copy(b, n).wait_send()
            r1_copy(n).wait_send()

        @pl.when(owner(n) != me)
        def _():
            for b in range(MICRO):
                a_copy(b, n).wait_send()
        return 0

    def members_sent(i, _):
        @pl.when(i != place)
        def _():
            for b in range(MICRO):
                for u in range(OWN_KV):
                    kv_copy(b, u, i).wait_send()
                    g_copy(b, u, i).wait_send()
            r2_copy(i).wait_send()
        return 0

    def reps_sent(i, _):
        @pl.when(i != rep)
        def _():
            r3_copy(i).wait_send()
        return 0

    lax.fori_loop(0, SAMPLES, heads_sent, 0)
    lax.fori_loop(0, TILES, members_sent, 0)
    lax.fori_loop(0, n_rep, reps_sent, 0)

    pltpu.make_async_copy(red3, red3, r3_recv.at[0]).wait()
    total = jnp.sum(red3[...], axis=0)
    dgain_ref[...] = total[0:1]
    dgate_ref[...] = jnp.broadcast_to(jnp.sum(total[1:2], axis=1, keepdims=True) * (1.0 - gate * gate), (1, HEAD))

    pltpu.make_async_copy(att_ref, att_ref, a_recv.at[0]).wait()
    pltpu.make_async_copy(dkv_ref, dkv_ref, g_recv.at[0]).wait()


def shards(key_value, key_gain, queries, tile_count, attn_gate, cotangent):
    n_rep = lax.axis_size("dp") * lax.axis_size("segment")
    vmem, anywhere = pl.BlockSpec(memory_space=pltpu.VMEM), pl.BlockSpec(memory_space=pl.ANY)
    hbm = pl.BlockSpec(memory_space=pltpu.HBM)
    dma = pltpu.SemaphoreType.DMA
    bf16, f32 = jnp.bfloat16, jnp.float32
    gain_row = key_gain.reshape(1, HEAD)
    key_value, gain_row, queries, tile_count, cotangent = (
        pltpu.with_memory_space_constraint(x, pltpu.HBM)
        for x in (key_value, gain_row, queries, tile_count, cotangent)
    )
    attended, d_key_value, d_gain, d_gate = pl.pallas_call(
        kernel,
        out_shape=(
            jax.ShapeDtypeStruct(queries.shape, bf16),
            jax.ShapeDtypeStruct(key_value.shape, bf16),
            jax.ShapeDtypeStruct((1, HEAD), f32),
            jax.ShapeDtypeStruct((1, HEAD), f32),
        ),
        in_specs=[hbm, hbm, hbm, hbm, pl.BlockSpec(memory_space=pltpu.SMEM), hbm],
        out_specs=(anywhere, anywhere, vmem, vmem),
        scratch_shapes=[
            pltpu.VMEM((MICRO, OWN_KV, TILES, PATCH, WIDE), bf16),
            pltpu.VMEM((MICRO, OWN_HEADS, TEXT, HEAD), bf16),
            pltpu.VMEM((MICRO, OWN_HEADS, TEXT, HEAD), bf16),
            pltpu.VMEM((MICRO, OWN_KV, TILES, PATCH, WIDE), bf16),
            pltpu.VMEM((MICRO, OWN_HEADS, TEXT, HEAD), bf16),
            pltpu.VMEM((ROWS, GROUP * HEAD), bf16),
            pltpu.VMEM((ROWS, GROUP * HEAD), bf16),
            pltpu.VMEM((3, 8, HEAD), f32),
            pltpu.VMEM((SAMPLES, 8, HEAD), f32),
            pltpu.VMEM((TILES, 8, HEAD), f32),
            pltpu.VMEM((n_rep, 8, HEAD), f32),
            dma((MICRO, OWN_KV, TILES)), dma((MICRO, OWN_KV)),
            dma((MICRO, SAMPLES)), dma((MICRO, OWN_KV)),
            dma((MICRO, SAMPLES)), dma((MICRO, OWN_KV)),
            dma((MICRO, OWN_KV, TILES)), dma((1,)),
            dma((MICRO, OWN_HEADS)), dma((1,)),
            dma((SAMPLES,)), dma((1,)), dma((TILES,)), dma((1,)), dma((n_rep,)), dma((1,)),
            pltpu.VMEM((1, HEAD), f32), pltpu.VMEM(tile_count.shape, jnp.int32), dma((2,)),
        ],
        compiler_params=pltpu.CompilerParams(
            collective_id=0, has_side_effects=True, vmem_limit_bytes=48 * 1024 * 1024
        ),
        name="cross_attention",
    )(key_value, gain_row, queries, tile_count, attn_gate, cotangent)
    return attended, d_key_value, d_gain.reshape(HEAD), d_gate[0, :1]


def solution(mesh):
    in_specs = (
        P("dp", ("segment", "mp"), None, None),
        P(),
        P("dp", "segment", None, "mp"),
        P("dp", "segment", None),
        P(),
        P("dp", "segment", None, "mp"),
    )
    out_specs = (P("dp", "segment", None, "mp"), P("dp", ("segment", "mp"), None, None), P(), P())
    return jax.shard_map(shards, mesh=mesh, in_specs=in_specs, out_specs=out_specs, check_vma=False)
```

```python
import jax
import jax.numpy as jnp
from jax import lax
from jax.experimental import pallas as pl
from jax.experimental.pallas import tpu as pltpu
from jax.sharding import PartitionSpec as P

HEAD = 128
TILES = 4
PATCH = 96
KEYS = TILES * PATCH
MICRO = 2
SAMPLES = 16
TEXT = 32
GROUP = 8
OWN_KV = 2
OWN_HEADS = OWN_KV * GROUP
ROWS = GROUP * TEXT
WIDE = 2 * HEAD
GRADS_AT_ONCE = 1
GRADS_AFTER = ((1,), (2, 3))
ORDER = (
    (((0, 0), (0, 1), (1, 0)), (), ((1, 1),)),
    (((0, 0),), (), ((0, 1), (1, 0), (1, 1))),
)
HOLD_A = 1
SCALE = 1.0 / HEAD**0.5


def dot(a, b, dims):
    return lax.dot_general(a, b, (dims, ((), ())), preferred_element_type=jnp.float32)


def kernel(
    kv_ref, gain_ref, q_ref, count_ref, gate_ref, cot_ref,
    att_ref, dkv_ref, dgain_ref, dgate_ref,
    kvbuf, qbuf, cbuf, gbuf, abuf, qblk, dblk, red_src, red_rep, red_plane,
    kv_send, kv_recv, q_send, q_recv, c_send, c_recv, g_send, g_recv, a_send, a_recv,
    rep_send, plane_send, sum_recv,
    gain_v, count_v, small_sem, go_sem, all_sem, rep_sem,
):
    me = lax.axis_index("mp")
    seg = lax.axis_index("segment")
    dp = lax.axis_index("dp")
    n_mp = lax.axis_size("mp")
    n_rep = lax.axis_size("dp") * lax.axis_size("segment")
    sample = me // TILES
    place = me % TILES
    part = (place + TILES - (sample // 2) % TILES) % TILES
    my_part = me // OWN_HEADS
    my_slot = me % OWN_HEADS
    my_unit = my_slot // GROUP
    rep = dp * lax.axis_size("segment") + seg

    def worker(n):
        return n * TILES + (my_part + n // 2) % TILES

    def owner(i):
        return part * OWN_HEADS + i

    def member(i):
        return sample * TILES + i

    def member_part(i):
        return (i + TILES - (sample // 2) % TILES) % TILES

    def turn(k):
        r = k // 2
        row = sample // 2 + 8 + ((r + 1) // 2) * (1 - 2 * (r % 2))
        return (row % 8) * 2 + (k + sample) % 2

    def other(k):
        return (place + 1 + k) % TILES

    def rep_id(i):
        return {"segment": i % lax.axis_size("segment"), "dp": i // lax.axis_size("segment")}

    smalls = [
        pltpu.make_async_copy(gain_ref, gain_v, small_sem.at[0]),
        pltpu.make_async_copy(count_ref, count_v, small_sem.at[1]),
    ]
    for copy in smalls:
        copy.start()

    barrier = pltpu.get_barrier_semaphore()

    def tell(sem, first):
        def step(k, _):
            pl.semaphore_signal(sem, inc=1, device_id={"mp": member((first + 1 + k) % TILES)})
            return 0
        lax.fori_loop(0, TILES - 1, step, 0)

    @pl.when(place == 0)
    def _():
        pl.semaphore_wait(barrier, TILES - 1)
        tell(go_sem, 0)

    @pl.when(place != 0)
    def _():
        pl.semaphore_signal(barrier, inc=1, device_id={"mp": member(0)})
        pl.semaphore_wait(go_sem, 1)

    def greet_samples(k, _):
        n = place * TILES + k

        @pl.when(n != sample)
        def _():
            pl.semaphore_signal(barrier, inc=1, device_id={"mp": n * TILES + 1})
        return 0

    lax.fori_loop(0, SAMPLES // TILES, greet_samples, 0)

    def wait_plane():
        @pl.when(place == 1)
        def _():
            pl.semaphore_wait(barrier, SAMPLES - 1)
            tell(all_sem, 1)

        @pl.when(place != 1)
        def _():
            pl.semaphore_wait(all_sem, 1)

    def greet_reps():
        def step(i, _):
            @pl.when(i != rep)
            def _():
                pl.semaphore_signal(barrier, inc=1, device_id=rep_id(i))
            return 0

        @pl.when(place == 2)
        def _():
            lax.fori_loop(0, n_rep, step, 0)

    def wait_reps():
        @pl.when(place == 2)
        def _():
            pl.semaphore_wait(barrier, n_rep - 1)
            tell(rep_sem, 2)

        @pl.when(place != 2)
        def _():
            pl.semaphore_wait(rep_sem, 1)

    def columns(p, u):
        return pl.ds(pl.multiple_of((p * OWN_KV + u) * WIDE, WIDE), WIDE)

    def kv_copy(b, u, i):
        return pltpu.make_async_remote_copy(
            kv_ref.at[b, 0, :, columns(member_part(i), u)], kvbuf.at[b, u, place],
            kv_send.at[b, u, i], kv_recv.at[b, u], device_id={"mp": member(i)},
        )

    def q_copy(b, n):
        return pltpu.make_async_remote_copy(
            q_ref.at[b, n], qbuf.at[b, my_slot], q_send.at[b, n], q_recv.at[b, my_unit],
            device_id={"mp": worker(n)},
        )

    def c_copy(b, n):
        return pltpu.make_async_remote_copy(
            cot_ref.at[b, n], cbuf.at[b, my_slot], c_send.at[b, n], c_recv.at[b, my_unit],
            device_id={"mp": worker(n)},
        )

    def send_kv(b, u):
        def step(k, _):
            kv_copy(b, u, other(k)).start()
            return 0
        lax.fori_loop(0, TILES - 1, step, 0)
        pltpu.make_async_copy(
            kv_ref.at[b, 0, :, columns(part, u)], kvbuf.at[b, u, place], kv_recv.at[b, u]
        ).start()

    def send_heads(b):
        def q_step(k, _):
            n = turn(k)

            @pl.when(worker(n) != me)
            def _():
                q_copy(b, n).start()

            @pl.when(worker(n) == me)
            def _():
                pltpu.make_async_copy(q_ref.at[b, n], qbuf.at[b, my_slot], q_recv.at[b, my_unit]).start()
            return 0

        def c_step(k, _):
            n = turn(k)

            @pl.when(worker(n) != me)
            def _():
                c_copy(b, n).start()

            @pl.when(worker(n) == me)
            def _():
                pltpu.make_async_copy(cot_ref.at[b, n], cbuf.at[b, my_slot], c_recv.at[b, my_unit]).start()
            return 0

        lax.fori_loop(0, SAMPLES, q_step, 0)
        lax.fori_loop(0, SAMPLES, c_step, 0)

    def send_units(units, when):
        @pl.when(when)
        def _():
            for b, u in units:
                send_kv(b, u)

    first_half = sample % 2 == 0
    for half, when in ((0, first_half), (1, jnp.logical_not(first_half))):
        send_units(ORDER[half][0], when)
    qblk[...] = jnp.zeros_like(qblk)
    dblk[...] = jnp.zeros_like(dblk)
    wait_plane()
    greet_reps()
    send_heads(0)
    for half, when in ((0, first_half), (1, jnp.logical_not(first_half))):
        send_units(ORDER[half][1], when)
    send_heads(1)
    for half, when in ((0, first_half), (1, jnp.logical_not(first_half))):
        send_units(ORDER[half][2], when)
    wait_reps()

    for copy in smalls:
        copy.wait()
    gate = jnp.tanh(jnp.full((1, HEAD), gate_ref[0], jnp.float32))
    gain = gain_v[...]
    token_of = (lax.broadcasted_iota(jnp.int32, (ROWS, TEXT), 0) & (TEXT - 1)) == (
        lax.broadcasted_iota(jnp.int32, (ROWS, TEXT), 1)
    )
    spread = token_of.astype(jnp.bfloat16)
    key_row = lax.broadcasted_iota(jnp.int32, (KEYS, ROWS), 0)

    def g_copy(b, u, i):
        return pltpu.make_async_remote_copy(
            gbuf.at[b, u, i], dkv_ref.at[b, 0, :, columns(part, u)], g_send.at[b, u, i], g_recv.at[0],
            device_id={"mp": member(i)},
        )

    def a_copy(b, i):
        return pltpu.make_async_remote_copy(
            abuf.at[b, i], att_ref.at[b, sample], a_send.at[b, i], a_recv.at[0],
            device_id={"mp": owner(i)},
        )

    def send_grads(b, u):
        def g_step(k, _):
            g_copy(b, u, other(k)).start()
            return 0

        lax.fori_loop(0, TILES - 1, g_step, 0)
        pltpu.make_async_copy(
            gbuf.at[b, u, place], dkv_ref.at[b, 0, :, columns(part, u)], g_recv.at[0]
        ).start()

    def send_attended(b, u):
        def a_step(k, _):
            i = u * GROUP + (k + me) % GROUP

            @pl.when(owner(i) != me)
            def _():
                a_copy(b, i).start()

            @pl.when(owner(i) == me)
            def _():
                pltpu.make_async_copy(abuf.at[b, i], att_ref.at[b, sample], a_recv.at[0]).start()
            return 0

        lax.fori_loop(0, GROUP, a_step, 0)

    def unit(step, carry):
        gain_sum, gate_sum = carry
        b = step // OWN_KV
        u = step % OWN_KV
        heads = pl.ds(u * GROUP, GROUP)
        q_view, c_view = qbuf.at[b, heads], cbuf.at[b, heads]
        counts = count_v[b, pl.ds(sample, 1), :].astype(jnp.float32).astype(jnp.bfloat16)
        count_col = dot(spread, jnp.broadcast_to(counts, (HEAD, TEXT)), ((1,), (1,)))
        count_row = dot(jnp.broadcast_to(counts, (8, TEXT)), spread, ((1,), (1,)))[0:1]
        live = (count_col > 0.5).astype(jnp.float32)
        gate_live = gate * live
        limit = (jnp.maximum(count_row, 1.0) * PATCH).astype(jnp.int32)

        pltpu.make_async_copy(kvbuf.at[b, u], kvbuf.at[b, u], kv_recv.at[b, u]).wait()
        kv = kvbuf[b, u].reshape(KEYS, WIDE)
        raw = kv[:, :HEAD].astype(jnp.float32)
        values = kv[:, HEAD:]
        inverse = lax.rsqrt(jnp.mean(raw * raw, axis=-1, keepdims=True) + 1e-05)
        unit_key = raw * inverse
        keys = (unit_key * gain).astype(jnp.bfloat16)

        pltpu.make_async_copy(q_view, q_view, q_recv.at[b, u]).wait()
        queries = q_view[...].reshape(ROWS, HEAD)
        logits = dot(keys, queries, ((1,), (1,))) * SCALE
        logits = jnp.where(key_row < limit, logits, -1e30)
        exps = jnp.exp(logits - jnp.max(logits, axis=0, keepdims=True))
        probs = exps / jnp.sum(exps, axis=0, keepdims=True)
        probs_low = probs.astype(jnp.bfloat16)
        mixed = dot(probs_low, values, ((0,), (0,)))
        abuf[b, heads] = (gate_live * mixed).astype(jnp.bfloat16).reshape(GROUP, TEXT, HEAD)

        @pl.when(step < MICRO * OWN_KV - HOLD_A)
        def _():
            send_attended(b, u)

        pltpu.make_async_copy(c_view, c_view, c_recv.at[b, u]).wait()
        cotan = c_view[...].reshape(ROWS, HEAD).astype(jnp.float32)
        gate_sum = gate_sum + jnp.sum(cotan * live * mixed, axis=0, keepdims=True)
        d_mixed = (gate_live * cotan).astype(jnp.bfloat16)
        d_probs = dot(values, d_mixed, ((1,), (1,)))
        inner = jnp.sum(probs * d_probs, axis=0, keepdims=True)
        d_logits = (probs * (d_probs - inner) * SCALE).astype(jnp.bfloat16)
        for h in range(GROUP):
            rows, cols = slice(h * TEXT, (h + 1) * TEXT), slice(h * HEAD, (h + 1) * HEAD)
            qblk[rows, cols] = queries[rows]
            dblk[rows, cols] = d_mixed[rows]

        def head_sum(left, blocks):
            total = jnp.zeros((KEYS, HEAD), jnp.float32)
            for h in range(0, GROUP, 2):
                pair = dot(left, blocks[:, h * HEAD:(h + 2) * HEAD], ((1,), (0,)))
                pair = pair.astype(jnp.bfloat16).astype(jnp.float32)
                total = total + pair[:, :HEAD] + pair[:, HEAD:]
            return total.astype(jnp.bfloat16)

        key_part = head_sum(d_logits, qblk).astype(jnp.float32)
        value_part = head_sum(probs_low, dblk)
        gain_sum = gain_sum + jnp.sum(key_part * unit_key, axis=0, keepdims=True)
        scaled = key_part * gain
        d_key = inverse * (scaled - unit_key * jnp.mean(scaled * unit_key, axis=-1, keepdims=True))
        gbuf[b, u, :, :, :HEAD] = d_key.astype(jnp.bfloat16).reshape(TILES, PATCH, HEAD)
        gbuf[b, u, :, :, HEAD:] = value_part.reshape(TILES, PATCH, HEAD)


        @pl.when(step < GRADS_AT_ONCE)
        def _():
            send_grads(b, u)

        return gain_sum, gate_sum

    zero = jnp.zeros((1, HEAD), jnp.float32)
    gain_sum, gate_sum = lax.fori_loop(0, MICRO * OWN_KV, unit, (zero, zero))

    red_src[0, 0:1] = gain_sum
    red_src[0, 1:2] = gate_sum

    def after_sums(i):
        for step in GRADS_AFTER[i]:
            send_grads(step // OWN_KV, step % OWN_KV)

    def rep_copy(k):
        return pltpu.make_async_remote_copy(
            red_src.at[0], red_rep.at[rep], rep_send.at[k], sum_recv.at[0], device_id=rep_id(k)
        )

    def plane_copy(k):
        return pltpu.make_async_remote_copy(
            red_src.at[1], red_plane.at[me], plane_send.at[k], sum_recv.at[1], device_id={"mp": (me + k) % n_mp}
        )

    def rep_step(k, _):
        @pl.when(k != rep)
        def _():
            rep_copy(k).start()
        return 0

    def plane_step(k, _):
        plane_copy(k).start()
        return 0

    lax.fori_loop(0, n_rep, rep_step, 0)
    pltpu.make_async_copy(red_src.at[0], red_rep.at[rep], sum_recv.at[0]).start()
    for step in range(MICRO * OWN_KV - HOLD_A, MICRO * OWN_KV):
        send_attended(step // OWN_KV, step % OWN_KV)
    after_sums(0)
    pltpu.make_async_copy(red_rep, red_rep, sum_recv.at[0]).wait()
    red_src[1] = jnp.sum(red_rep[...], axis=0)
    pltpu.make_async_copy(red_src.at[1], red_plane.at[me], sum_recv.at[1]).start()
    lax.fori_loop(1, n_mp, plane_step, 0)
    after_sums(1)

    def heads_sent(n, _):
        @pl.when(worker(n) != me)
        def _():
            for b in range(MICRO):
                q_copy(b, n).wait_send()
                c_copy(b, n).wait_send()

        @pl.when(owner(n) != me)
        def _():
            for b in range(MICRO):
                a_copy(b, n).wait_send()
        return 0

    def members_sent(i, _):
        @pl.when(i != place)
        def _():
            for b in range(MICRO):
                for u in range(OWN_KV):
                    kv_copy(b, u, i).wait_send()
                    g_copy(b, u, i).wait_send()
        return 0

    def reps_sent(k, _):
        @pl.when(k != rep)
        def _():
            rep_copy(k).wait_send()
        return 0

    def plane_sent(k, _):
        plane_copy(k).wait_send()
        return 0

    lax.fori_loop(0, SAMPLES, heads_sent, 0)
    lax.fori_loop(0, TILES, members_sent, 0)
    lax.fori_loop(0, n_rep, reps_sent, 0)
    lax.fori_loop(1, n_mp, plane_sent, 0)

    pltpu.make_async_copy(red_plane, red_plane, sum_recv.at[1]).wait()
    total = jnp.sum(red_plane[...], axis=0)
    dgain_ref[...] = total[0:1]
    dgate_ref[...] = jnp.broadcast_to(jnp.sum(total[1:2], axis=1, keepdims=True) * (1.0 - gate * gate), (1, HEAD))

    pltpu.make_async_copy(att_ref, att_ref, a_recv.at[0]).wait()
    pltpu.make_async_copy(dkv_ref, dkv_ref, g_recv.at[0]).wait()


def shards(key_value, key_gain, queries, tile_count, attn_gate, cotangent):
    n_rep = lax.axis_size("dp") * lax.axis_size("segment")
    n_mp = lax.axis_size("mp")
    vmem, anywhere = pl.BlockSpec(memory_space=pltpu.VMEM), pl.BlockSpec(memory_space=pl.ANY)
    hbm = pl.BlockSpec(memory_space=pltpu.HBM)
    dma = pltpu.SemaphoreType.DMA
    bf16, f32 = jnp.bfloat16, jnp.float32
    gain_row = key_gain.reshape(1, HEAD)
    key_value, gain_row, queries, tile_count, cotangent = (
        pltpu.with_memory_space_constraint(x, pltpu.HBM)
        for x in (key_value, gain_row, queries, tile_count, cotangent)
    )
    attended, d_key_value, d_gain, d_gate = pl.pallas_call(
        kernel,
        out_shape=(
            jax.ShapeDtypeStruct(queries.shape, bf16),
            jax.ShapeDtypeStruct(key_value.shape, bf16),
            jax.ShapeDtypeStruct((1, HEAD), f32),
            jax.ShapeDtypeStruct((1, HEAD), f32),
        ),
        in_specs=[hbm, hbm, hbm, hbm, pl.BlockSpec(memory_space=pltpu.SMEM), hbm],
        out_specs=(anywhere, anywhere, vmem, vmem),
        scratch_shapes=[
            pltpu.VMEM((MICRO, OWN_KV, TILES, PATCH, WIDE), bf16),
            pltpu.VMEM((MICRO, OWN_HEADS, TEXT, HEAD), bf16),
            pltpu.VMEM((MICRO, OWN_HEADS, TEXT, HEAD), bf16),
            pltpu.VMEM((MICRO, OWN_KV, TILES, PATCH, WIDE), bf16),
            pltpu.VMEM((MICRO, OWN_HEADS, TEXT, HEAD), bf16),
            pltpu.VMEM((ROWS, GROUP * HEAD), bf16),
            pltpu.VMEM((ROWS, GROUP * HEAD), bf16),
            pltpu.VMEM((2, 2, HEAD), f32),
            pltpu.VMEM((n_rep, 2, HEAD), f32),
            pltpu.VMEM((n_mp, 2, HEAD), f32),
            dma((MICRO, OWN_KV, TILES)), dma((MICRO, OWN_KV)),
            dma((MICRO, SAMPLES)), dma((MICRO, OWN_KV)),
            dma((MICRO, SAMPLES)), dma((MICRO, OWN_KV)),
            dma((MICRO, OWN_KV, TILES)), dma((1,)),
            dma((MICRO, OWN_HEADS)), dma((1,)),
            dma((n_rep,)), dma((n_mp,)), dma((2,)),
            pltpu.VMEM((1, HEAD), f32), pltpu.VMEM(tile_count.shape, jnp.int32), dma((2,)),
            pltpu.SemaphoreType.REGULAR, pltpu.SemaphoreType.REGULAR, pltpu.SemaphoreType.REGULAR,
        ],
        compiler_params=pltpu.CompilerParams(
            collective_id=0, has_side_effects=True, vmem_limit_bytes=48 * 1024 * 1024
        ),
        name="cross_attention",
    )(key_value, gain_row, queries, tile_count, attn_gate, cotangent)
    return attended, d_key_value, d_gain.reshape(HEAD), d_gate[0, :1]


def solution(mesh):
    in_specs = (
        P("dp", ("segment", "mp"), None, None),
        P(),
        P("dp", "segment", None, "mp"),
        P("dp", "segment", None),
        P(),
        P("dp", "segment", None, "mp"),
    )
    out_specs = (P("dp", "segment", None, "mp"), P("dp", ("segment", "mp"), None, None), P(), P())
    return jax.shard_map(shards, mesh=mesh, in_specs=in_specs, out_specs=out_specs, check_vma=False)
```

```python
import jax
import jax.numpy as jnp
from jax import lax
from jax.experimental import pallas as pl
from jax.experimental.pallas import tpu as pltpu
from jax.sharding import PartitionSpec as P

HEAD = 128
TILES = 4
PATCH = 96
KEYS = TILES * PATCH
MICRO = 2
SAMPLES = 16
TEXT = 32
GROUP = 8
OWN_KV = 2
OWN_HEADS = OWN_KV * GROUP
ROWS = GROUP * TEXT
WIDE = 2 * HEAD
GRADS_AT_ONCE = 1
GRADS_AFTER = ((1,), (2, 3))
ORDER = (
    (((0, 0), (0, 1)), ((1, 0),), ((1, 1),)),
    (((0, 0),), ((0, 1),), ((1, 0), (1, 1))),
)
HOLD_A = 1
SCALE = 1.0 / HEAD**0.5


def dot(a, b, dims):
    return lax.dot_general(a, b, (dims, ((), ())), preferred_element_type=jnp.float32)


def kernel(
    kv_ref, gain_ref, q_ref, count_ref, gate_ref, cot_ref,
    att_ref, dkv_ref, dgain_ref, dgate_ref,
    kvbuf, qbuf, cbuf, gbuf, abuf, qblk, dblk, red_src, red_rep, red_plane,
    kv_send, kv_recv, q_send, q_recv, c_send, c_recv, g_send, g_recv, a_send, a_recv,
    rep_send, plane_send, sum_recv,
    gain_v, count_v, small_sem, go_sem, all_sem, rep_sem,
):
    me = lax.axis_index("mp")
    seg = lax.axis_index("segment")
    dp = lax.axis_index("dp")
    n_mp = lax.axis_size("mp")
    n_rep = lax.axis_size("dp") * lax.axis_size("segment")
    sample = me // TILES
    place = me % TILES
    part = (place + TILES - (sample // 2) % TILES) % TILES
    my_part = me // OWN_HEADS
    my_slot = me % OWN_HEADS
    my_unit = my_slot // GROUP
    rep = dp * lax.axis_size("segment") + seg

    def worker(n):
        return n * TILES + (my_part + n // 2) % TILES

    def owner(i):
        return part * OWN_HEADS + i

    def member(i):
        return sample * TILES + i

    def member_part(i):
        return (i + TILES - (sample // 2) % TILES) % TILES

    def turn(k):
        r = k // 2
        row = sample // 2 + 8 + ((r + 1) // 2) * (1 - 2 * (r % 2))
        return (row % 8) * 2 + (k + sample) % 2

    def other(k):
        return (place + 1 + k) % TILES

    def rep_id(i):
        return {"segment": i % lax.axis_size("segment"), "dp": i // lax.axis_size("segment")}

    smalls = [
        pltpu.make_async_copy(gain_ref, gain_v, small_sem.at[0]),
        pltpu.make_async_copy(count_ref, count_v, small_sem.at[1]),
    ]
    for copy in smalls:
        copy.start()

    barrier = pltpu.get_barrier_semaphore()

    def tell(sem, first):
        def step(k, _):
            pl.semaphore_signal(sem, inc=1, device_id={"mp": member((first + 1 + k) % TILES)})
            return 0
        lax.fori_loop(0, TILES - 1, step, 0)

    @pl.when(place == 0)
    def _():
        pl.semaphore_wait(barrier, TILES - 1)
        tell(go_sem, 0)

    @pl.when(place != 0)
    def _():
        pl.semaphore_signal(barrier, inc=1, device_id={"mp": member(0)})
        pl.semaphore_wait(go_sem, 1)

    def greet_samples(k, _):
        n = place * TILES + k

        @pl.when(n != sample)
        def _():
            pl.semaphore_signal(barrier, inc=1, device_id={"mp": n * TILES + 1})
        return 0

    lax.fori_loop(0, SAMPLES // TILES, greet_samples, 0)

    def wait_plane():
        @pl.when(place == 1)
        def _():
            pl.semaphore_wait(barrier, SAMPLES - 1)
            tell(all_sem, 1)

        @pl.when(place != 1)
        def _():
            pl.semaphore_wait(all_sem, 1)

    def greet_reps():
        def step(i, _):
            @pl.when(i != rep)
            def _():
                pl.semaphore_signal(barrier, inc=1, device_id=rep_id(i))
            return 0

        @pl.when(place == 2)
        def _():
            lax.fori_loop(0, n_rep, step, 0)

    def wait_reps():
        @pl.when(place == 2)
        def _():
            pl.semaphore_wait(barrier, n_rep - 1)
            tell(rep_sem, 2)

        @pl.when(place != 2)
        def _():
            pl.semaphore_wait(rep_sem, 1)

    def columns(p, u):
        return pl.ds(pl.multiple_of((p * OWN_KV + u) * WIDE, WIDE), WIDE)

    def kv_copy(b, u, i):
        return pltpu.make_async_remote_copy(
            kv_ref.at[b, 0, :, columns(member_part(i), u)], kvbuf.at[b, u, place],
            kv_send.at[b, u, i], kv_recv.at[b, u], device_id={"mp": member(i)},
        )

    def q_copy(b, n):
        return pltpu.make_async_remote_copy(
            q_ref.at[b, n], qbuf.at[b, my_slot], q_send.at[b, n], q_recv.at[b, my_unit],
            device_id={"mp": worker(n)},
        )

    def c_copy(b, n):
        return pltpu.make_async_remote_copy(
            cot_ref.at[b, n], cbuf.at[b, my_slot], c_send.at[b, n], c_recv.at[b, my_unit],
            device_id={"mp": worker(n)},
        )

    def send_kv(b, u):
        def step(k, _):
            kv_copy(b, u, other(k)).start()
            return 0
        lax.fori_loop(0, TILES - 1, step, 0)
        pltpu.make_async_copy(
            kv_ref.at[b, 0, :, columns(part, u)], kvbuf.at[b, u, place], kv_recv.at[b, u]
        ).start()

    def send_heads(b):
        def q_step(k, _):
            n = turn(k)

            @pl.when(worker(n) != me)
            def _():
                q_copy(b, n).start()

            @pl.when(worker(n) == me)
            def _():
                pltpu.make_async_copy(q_ref.at[b, n], qbuf.at[b, my_slot], q_recv.at[b, my_unit]).start()
            return 0

        def c_step(k, _):
            n = turn(k)

            @pl.when(worker(n) != me)
            def _():
                c_copy(b, n).start()

            @pl.when(worker(n) == me)
            def _():
                pltpu.make_async_copy(cot_ref.at[b, n], cbuf.at[b, my_slot], c_recv.at[b, my_unit]).start()
            return 0

        lax.fori_loop(0, SAMPLES, q_step, 0)
        lax.fori_loop(0, SAMPLES, c_step, 0)

    def send_units(units, when):
        @pl.when(when)
        def _():
            for b, u in units:
                send_kv(b, u)

    first_half = sample % 2 == 0
    for half, when in ((0, first_half), (1, jnp.logical_not(first_half))):
        send_units(ORDER[half][0], when)
    qblk[...] = jnp.zeros_like(qblk)
    dblk[...] = jnp.zeros_like(dblk)
    wait_plane()
    greet_reps()
    send_heads(0)
    for half, when in ((0, first_half), (1, jnp.logical_not(first_half))):
        send_units(ORDER[half][1], when)
    send_heads(1)
    for half, when in ((0, first_half), (1, jnp.logical_not(first_half))):
        send_units(ORDER[half][2], when)
    wait_reps()

    for copy in smalls:
        copy.wait()
    gate = jnp.tanh(jnp.full((1, HEAD), gate_ref[0], jnp.float32))
    gain = gain_v[...]
    token_of = (lax.broadcasted_iota(jnp.int32, (ROWS, TEXT), 0) & (TEXT - 1)) == (
        lax.broadcasted_iota(jnp.int32, (ROWS, TEXT), 1)
    )
    spread = token_of.astype(jnp.bfloat16)
    key_row = lax.broadcasted_iota(jnp.int32, (KEYS, ROWS), 0)

    def g_copy(b, u, i):
        return pltpu.make_async_remote_copy(
            gbuf.at[b, u, i], dkv_ref.at[b, 0, :, columns(part, u)], g_send.at[b, u, i], g_recv.at[0],
            device_id={"mp": member(i)},
        )

    def a_copy(b, i):
        return pltpu.make_async_remote_copy(
            abuf.at[b, i], att_ref.at[b, sample], a_send.at[b, i], a_recv.at[0],
            device_id={"mp": owner(i)},
        )

    def send_grads(b, u):
        def g_step(k, _):
            g_copy(b, u, other(k)).start()
            return 0

        lax.fori_loop(0, TILES - 1, g_step, 0)
        pltpu.make_async_copy(
            gbuf.at[b, u, place], dkv_ref.at[b, 0, :, columns(part, u)], g_recv.at[0]
        ).start()

    def send_attended(b, u):
        def a_step(k, _):
            i = u * GROUP + (k + me) % GROUP

            @pl.when(owner(i) != me)
            def _():
                a_copy(b, i).start()

            @pl.when(owner(i) == me)
            def _():
                pltpu.make_async_copy(abuf.at[b, i], att_ref.at[b, sample], a_recv.at[0]).start()
            return 0

        lax.fori_loop(0, GROUP, a_step, 0)

    def rep_copy(k):
        return pltpu.make_async_remote_copy(
            red_src.at[0], red_rep.at[rep], rep_send.at[k], sum_recv.at[0], device_id=rep_id(k)
        )

    def plane_copy(k):
        return pltpu.make_async_remote_copy(
            red_src.at[1], red_plane.at[me], plane_send.at[k], sum_recv.at[1], device_id={"mp": (me + k) % n_mp}
        )

    def rep_step(k, _):
        @pl.when(k != rep)
        def _():
            rep_copy(k).start()
        return 0

    def send_sums(gain_sum, gate_sum):
        red_src[0, 0:1] = gain_sum
        red_src[0, 1:2] = gate_sum
        lax.fori_loop(0, n_rep, rep_step, 0)
        pltpu.make_async_copy(red_src.at[0], red_rep.at[rep], sum_recv.at[0]).start()

    def unit(step, carry):
        gain_sum, gate_sum = carry
        b = step // OWN_KV
        u = step % OWN_KV
        heads = pl.ds(u * GROUP, GROUP)
        q_view, c_view = qbuf.at[b, heads], cbuf.at[b, heads]
        counts = count_v[b, pl.ds(sample, 1), :].astype(jnp.float32).astype(jnp.bfloat16)
        count_col = dot(spread, jnp.broadcast_to(counts, (HEAD, TEXT)), ((1,), (1,)))
        count_row = dot(jnp.broadcast_to(counts, (8, TEXT)), spread, ((1,), (1,)))[0:1]
        live = (count_col > 0.5).astype(jnp.float32)
        gate_live = gate * live
        limit = (jnp.maximum(count_row, 1.0) * PATCH).astype(jnp.int32)

        pltpu.make_async_copy(kvbuf.at[b, u], kvbuf.at[b, u], kv_recv.at[b, u]).wait()
        kv = kvbuf[b, u].reshape(KEYS, WIDE)
        raw = kv[:, :HEAD].astype(jnp.float32)
        values = kv[:, HEAD:]
        inverse = lax.rsqrt(jnp.mean(raw * raw, axis=-1, keepdims=True) + 1e-05)
        unit_key = raw * inverse
        keys = (unit_key * gain).astype(jnp.bfloat16)

        pltpu.make_async_copy(q_view, q_view, q_recv.at[b, u]).wait()
        queries = q_view[...].reshape(ROWS, HEAD)
        logits = dot(keys, queries, ((1,), (1,))) * SCALE
        logits = jnp.where(key_row < limit, logits, -1e30)
        exps = jnp.exp(logits - jnp.max(logits, axis=0, keepdims=True))
        probs = exps / jnp.sum(exps, axis=0, keepdims=True)
        probs_low = probs.astype(jnp.bfloat16)
        mixed = dot(probs_low, values, ((0,), (0,)))
        abuf[b, heads] = (gate_live * mixed).astype(jnp.bfloat16).reshape(GROUP, TEXT, HEAD)

        @pl.when(step < MICRO * OWN_KV - HOLD_A)
        def _():
            send_attended(b, u)

        pltpu.make_async_copy(c_view, c_view, c_recv.at[b, u]).wait()
        cotan = c_view[...].reshape(ROWS, HEAD).astype(jnp.float32)
        gate_sum = gate_sum + jnp.sum(cotan * live * mixed, axis=0, keepdims=True)
        d_mixed = (gate_live * cotan).astype(jnp.bfloat16)
        d_probs = dot(values, d_mixed, ((1,), (1,)))
        inner = jnp.sum(probs * d_probs, axis=0, keepdims=True)
        d_logits = (probs * (d_probs - inner) * SCALE).astype(jnp.bfloat16)
        for h in range(GROUP):
            rows, cols = slice(h * TEXT, (h + 1) * TEXT), slice(h * HEAD, (h + 1) * HEAD)
            qblk[rows, cols] = queries[rows]
            dblk[rows, cols] = d_mixed[rows]

        def head_sum(left, blocks):
            total = jnp.zeros((KEYS, HEAD), jnp.float32)
            for h in range(0, GROUP, 2):
                pair = dot(left, blocks[:, h * HEAD:(h + 2) * HEAD], ((1,), (0,)))
                pair = pair.astype(jnp.bfloat16).astype(jnp.float32)
                total = total + pair[:, :HEAD] + pair[:, HEAD:]
            return total.astype(jnp.bfloat16)

        key_part = head_sum(d_logits, qblk).astype(jnp.float32)
        gain_sum = gain_sum + jnp.sum(key_part * unit_key, axis=0, keepdims=True)

        @pl.when(step == MICRO * OWN_KV - 1)
        def _():
            send_sums(gain_sum, gate_sum)

        value_part = head_sum(probs_low, dblk)
        scaled = key_part * gain
        d_key = inverse * (scaled - unit_key * jnp.mean(scaled * unit_key, axis=-1, keepdims=True))
        gbuf[b, u, :, :, :HEAD] = d_key.astype(jnp.bfloat16).reshape(TILES, PATCH, HEAD)
        gbuf[b, u, :, :, HEAD:] = value_part.reshape(TILES, PATCH, HEAD)


        @pl.when(step < GRADS_AT_ONCE)
        def _():
            send_grads(b, u)

        return gain_sum, gate_sum

    zero = jnp.zeros((1, HEAD), jnp.float32)
    lax.fori_loop(0, MICRO * OWN_KV, unit, (zero, zero))

    def after_sums(i):
        for step in GRADS_AFTER[i]:
            send_grads(step // OWN_KV, step % OWN_KV)

    def plane_step(k, _):
        plane_copy(k).start()
        return 0

    for step in range(MICRO * OWN_KV - HOLD_A, MICRO * OWN_KV):
        send_attended(step // OWN_KV, step % OWN_KV)
    after_sums(0)
    pltpu.make_async_copy(red_rep, red_rep, sum_recv.at[0]).wait()
    red_src[1] = jnp.sum(red_rep[...], axis=0)
    pltpu.make_async_copy(red_src.at[1], red_plane.at[me], sum_recv.at[1]).start()
    lax.fori_loop(1, n_mp, plane_step, 0)
    after_sums(1)

    def heads_sent(n, _):
        @pl.when(worker(n) != me)
        def _():
            for b in range(MICRO):
                q_copy(b, n).wait_send()
                c_copy(b, n).wait_send()

        @pl.when(owner(n) != me)
        def _():
            for b in range(MICRO):
                a_copy(b, n).wait_send()
        return 0

    def members_sent(i, _):
        @pl.when(i != place)
        def _():
            for b in range(MICRO):
                for u in range(OWN_KV):
                    kv_copy(b, u, i).wait_send()
                    g_copy(b, u, i).wait_send()
        return 0

    def reps_sent(k, _):
        @pl.when(k != rep)
        def _():
            rep_copy(k).wait_send()
        return 0

    def plane_sent(k, _):
        plane_copy(k).wait_send()
        return 0

    lax.fori_loop(0, SAMPLES, heads_sent, 0)
    lax.fori_loop(0, TILES, members_sent, 0)
    lax.fori_loop(0, n_rep, reps_sent, 0)
    lax.fori_loop(1, n_mp, plane_sent, 0)

    pltpu.make_async_copy(red_plane, red_plane, sum_recv.at[1]).wait()
    total = jnp.sum(red_plane[...], axis=0)
    dgain_ref[...] = total[0:1]
    dgate_ref[...] = jnp.broadcast_to(jnp.sum(total[1:2], axis=1, keepdims=True) * (1.0 - gate * gate), (1, HEAD))

    pltpu.make_async_copy(att_ref, att_ref, a_recv.at[0]).wait()
    pltpu.make_async_copy(dkv_ref, dkv_ref, g_recv.at[0]).wait()


def shards(key_value, key_gain, queries, tile_count, attn_gate, cotangent):
    n_rep = lax.axis_size("dp") * lax.axis_size("segment")
    n_mp = lax.axis_size("mp")
    vmem, anywhere = pl.BlockSpec(memory_space=pltpu.VMEM), pl.BlockSpec(memory_space=pl.ANY)
    hbm = pl.BlockSpec(memory_space=pltpu.HBM)
    dma = pltpu.SemaphoreType.DMA
    bf16, f32 = jnp.bfloat16, jnp.float32
    gain_row = key_gain.reshape(1, HEAD)
    key_value, gain_row, queries, tile_count, cotangent = (
        pltpu.with_memory_space_constraint(x, pltpu.HBM)
        for x in (key_value, gain_row, queries, tile_count, cotangent)
    )
    attended, d_key_value, d_gain, d_gate = pl.pallas_call(
        kernel,
        out_shape=(
            jax.ShapeDtypeStruct(queries.shape, bf16),
            jax.ShapeDtypeStruct(key_value.shape, bf16),
            jax.ShapeDtypeStruct((1, HEAD), f32),
            jax.ShapeDtypeStruct((1, HEAD), f32),
        ),
        in_specs=[hbm, hbm, hbm, hbm, pl.BlockSpec(memory_space=pltpu.SMEM), hbm],
        out_specs=(anywhere, anywhere, vmem, vmem),
        scratch_shapes=[
            pltpu.VMEM((MICRO, OWN_KV, TILES, PATCH, WIDE), bf16),
            pltpu.VMEM((MICRO, OWN_HEADS, TEXT, HEAD), bf16),
            pltpu.VMEM((MICRO, OWN_HEADS, TEXT, HEAD), bf16),
            pltpu.VMEM((MICRO, OWN_KV, TILES, PATCH, WIDE), bf16),
            pltpu.VMEM((MICRO, OWN_HEADS, TEXT, HEAD), bf16),
            pltpu.VMEM((ROWS, GROUP * HEAD), bf16),
            pltpu.VMEM((ROWS, GROUP * HEAD), bf16),
            pltpu.VMEM((2, 2, HEAD), f32),
            pltpu.VMEM((n_rep, 2, HEAD), f32),
            pltpu.VMEM((n_mp, 2, HEAD), f32),
            dma((MICRO, OWN_KV, TILES)), dma((MICRO, OWN_KV)),
            dma((MICRO, SAMPLES)), dma((MICRO, OWN_KV)),
            dma((MICRO, SAMPLES)), dma((MICRO, OWN_KV)),
            dma((MICRO, OWN_KV, TILES)), dma((1,)),
            dma((MICRO, OWN_HEADS)), dma((1,)),
            dma((n_rep,)), dma((n_mp,)), dma((2,)),
            pltpu.VMEM((1, HEAD), f32), pltpu.VMEM(tile_count.shape, jnp.int32), dma((2,)),
            pltpu.SemaphoreType.REGULAR, pltpu.SemaphoreType.REGULAR, pltpu.SemaphoreType.REGULAR,
        ],
        compiler_params=pltpu.CompilerParams(
            collective_id=0, has_side_effects=True, vmem_limit_bytes=48 * 1024 * 1024
        ),
        name="cross_attention",
    )(key_value, gain_row, queries, tile_count, attn_gate, cotangent)
    return attended, d_key_value, d_gain.reshape(HEAD), d_gate[0, :1]


def solution(mesh):
    in_specs = (
        P("dp", ("segment", "mp"), None, None),
        P(),
        P("dp", "segment", None, "mp"),
        P("dp", "segment", None),
        P(),
        P("dp", "segment", None, "mp"),
    )
    out_specs = (P("dp", "segment", None, "mp"), P("dp", ("segment", "mp"), None, None), P(), P())
    return jax.shard_map(shards, mesh=mesh, in_specs=in_specs, out_specs=out_specs, check_vma=False)
```

```python
import jax
import jax.numpy as jnp
from jax import lax
from jax.experimental import pallas as pl
from jax.experimental.pallas import tpu as pltpu
from jax.sharding import PartitionSpec as P

HEAD = 128
TILES = 4
PATCH = 96
KEYS = TILES * PATCH
MICRO = 2
SAMPLES = 16
TEXT = 32
GROUP = 8
OWN_KV = 2
OWN_HEADS = OWN_KV * GROUP
ROWS = GROUP * TEXT
WIDE = 2 * HEAD
GRADS_AT_ONCE = (2, 1)
GRADS_AFTER = (((), (2, 3)), ((1,), (2, 3)))
ORDER = (
    (((0, 0), (0, 1)), ((1, 0),), ((1, 1),)),
    (((0, 0),), ((0, 1),), ((1, 0), (1, 1))),
)
HOLD_A = 1
SCALE = 1.0 / HEAD**0.5


def dot(a, b, dims):
    return lax.dot_general(a, b, (dims, ((), ())), preferred_element_type=jnp.float32)


def kernel(
    kv_ref, gain_ref, q_ref, count_ref, gate_ref, cot_ref,
    att_ref, dkv_ref, dgain_ref, dgate_ref,
    kvbuf, qbuf, cbuf, gbuf, abuf, qblk, dblk, red_src, red_rep, red_plane,
    kv_send, kv_recv, q_send, q_recv, c_send, c_recv, g_send, g_recv, a_send, a_recv,
    rep_send, plane_send, sum_recv,
    gain_v, count_v, small_sem, go_sem, all_sem, rep_sem,
):
    me = lax.axis_index("mp")
    seg = lax.axis_index("segment")
    dp = lax.axis_index("dp")
    n_mp = lax.axis_size("mp")
    n_rep = lax.axis_size("dp") * lax.axis_size("segment")
    sample = me // TILES
    place = me % TILES
    part = (place + TILES - (sample // 2) % TILES) % TILES
    my_part = me // OWN_HEADS
    my_slot = me % OWN_HEADS
    my_unit = my_slot // GROUP
    rep = dp * lax.axis_size("segment") + seg

    def worker(n):
        return n * TILES + (my_part + n // 2) % TILES

    def owner(i):
        return part * OWN_HEADS + i

    def member(i):
        return sample * TILES + i

    def member_part(i):
        return (i + TILES - (sample // 2) % TILES) % TILES

    def turn(k):
        r = k // 2
        row = sample // 2 + 8 + ((r + 1) // 2) * (1 - 2 * (r % 2))
        return (row % 8) * 2 + (k + sample) % 2

    def other(k):
        return (place + 1 + k) % TILES

    def rep_id(i):
        return {"segment": i % lax.axis_size("segment"), "dp": i // lax.axis_size("segment")}

    smalls = [
        pltpu.make_async_copy(gain_ref, gain_v, small_sem.at[0]),
        pltpu.make_async_copy(count_ref, count_v, small_sem.at[1]),
    ]
    for copy in smalls:
        copy.start()

    barrier = pltpu.get_barrier_semaphore()

    def tell(sem, first):
        def step(k, _):
            pl.semaphore_signal(sem, inc=1, device_id={"mp": member((first + 1 + k) % TILES)})
            return 0
        lax.fori_loop(0, TILES - 1, step, 0)

    @pl.when(place == 0)
    def _():
        pl.semaphore_wait(barrier, TILES - 1)
        tell(go_sem, 0)

    @pl.when(place != 0)
    def _():
        pl.semaphore_signal(barrier, inc=1, device_id={"mp": member(0)})
        pl.semaphore_wait(go_sem, 1)

    def greet_samples(k, _):
        n = place * TILES + k

        @pl.when(n != sample)
        def _():
            pl.semaphore_signal(barrier, inc=1, device_id={"mp": n * TILES + 1})
        return 0

    lax.fori_loop(0, SAMPLES // TILES, greet_samples, 0)

    def wait_plane():
        @pl.when(place == 1)
        def _():
            pl.semaphore_wait(barrier, SAMPLES - 1)
            tell(all_sem, 1)

        @pl.when(place != 1)
        def _():
            pl.semaphore_wait(all_sem, 1)

    def greet_reps():
        def step(i, _):
            @pl.when(i != rep)
            def _():
                pl.semaphore_signal(barrier, inc=1, device_id=rep_id(i))
            return 0

        @pl.when(place == 2)
        def _():
            lax.fori_loop(0, n_rep, step, 0)

    def wait_reps():
        @pl.when(place == 2)
        def _():
            pl.semaphore_wait(barrier, n_rep - 1)
            tell(rep_sem, 2)

        @pl.when(place != 2)
        def _():
            pl.semaphore_wait(rep_sem, 1)

    def columns(p, u):
        return pl.ds(pl.multiple_of((p * OWN_KV + u) * WIDE, WIDE), WIDE)

    def kv_copy(b, u, i):
        return pltpu.make_async_remote_copy(
            kv_ref.at[b, 0, :, columns(member_part(i), u)], kvbuf.at[b, u, place],
            kv_send.at[b, u, i], kv_recv.at[b, u], device_id={"mp": member(i)},
        )

    def q_copy(b, n):
        return pltpu.make_async_remote_copy(
            q_ref.at[b, n], qbuf.at[b, my_slot], q_send.at[b, n], q_recv.at[b, my_unit],
            device_id={"mp": worker(n)},
        )

    def c_copy(b, n):
        return pltpu.make_async_remote_copy(
            cot_ref.at[b, n], cbuf.at[b, my_slot], c_send.at[b, n], c_recv.at[b, my_unit],
            device_id={"mp": worker(n)},
        )

    def send_kv(b, u):
        def step(k, _):
            kv_copy(b, u, other(k)).start()
            return 0
        lax.fori_loop(0, TILES - 1, step, 0)
        pltpu.make_async_copy(
            kv_ref.at[b, 0, :, columns(part, u)], kvbuf.at[b, u, place], kv_recv.at[b, u]
        ).start()

    def send_heads(b):
        def q_step(k, _):
            n = turn(k)

            @pl.when(worker(n) != me)
            def _():
                q_copy(b, n).start()

            @pl.when(worker(n) == me)
            def _():
                pltpu.make_async_copy(q_ref.at[b, n], qbuf.at[b, my_slot], q_recv.at[b, my_unit]).start()
            return 0

        def c_step(k, _):
            n = turn(k)

            @pl.when(worker(n) != me)
            def _():
                c_copy(b, n).start()

            @pl.when(worker(n) == me)
            def _():
                pltpu.make_async_copy(cot_ref.at[b, n], cbuf.at[b, my_slot], c_recv.at[b, my_unit]).start()
            return 0

        lax.fori_loop(0, SAMPLES, q_step, 0)
        lax.fori_loop(0, SAMPLES, c_step, 0)

    def send_units(units, when):
        @pl.when(when)
        def _():
            for b, u in units:
                send_kv(b, u)

    first_half = sample % 2 == 0
    for half, when in ((0, first_half), (1, jnp.logical_not(first_half))):
        send_units(ORDER[half][0], when)
    qblk[...] = jnp.zeros_like(qblk)
    dblk[...] = jnp.zeros_like(dblk)
    wait_plane()
    greet_reps()
    send_heads(0)
    for half, when in ((0, first_half), (1, jnp.logical_not(first_half))):
        send_units(ORDER[half][1], when)
    send_heads(1)
    for half, when in ((0, first_half), (1, jnp.logical_not(first_half))):
        send_units(ORDER[half][2], when)
    wait_reps()

    for copy in smalls:
        copy.wait()
    gate = jnp.tanh(jnp.full((1, HEAD), gate_ref[0], jnp.float32))
    gain = gain_v[...]
    token_of = (lax.broadcasted_iota(jnp.int32, (ROWS, TEXT), 0) & (TEXT - 1)) == (
        lax.broadcasted_iota(jnp.int32, (ROWS, TEXT), 1)
    )
    spread = token_of.astype(jnp.bfloat16)
    key_row = lax.broadcasted_iota(jnp.int32, (KEYS, ROWS), 0)

    def g_copy(b, u, i):
        return pltpu.make_async_remote_copy(
            gbuf.at[b, u, i], dkv_ref.at[b, 0, :, columns(part, u)], g_send.at[b, u, i], g_recv.at[0],
            device_id={"mp": member(i)},
        )

    def a_copy(b, i):
        return pltpu.make_async_remote_copy(
            abuf.at[b, i], att_ref.at[b, sample], a_send.at[b, i], a_recv.at[0],
            device_id={"mp": owner(i)},
        )

    def send_grads(b, u):
        def g_step(k, _):
            g_copy(b, u, other(k)).start()
            return 0

        lax.fori_loop(0, TILES - 1, g_step, 0)
        pltpu.make_async_copy(
            gbuf.at[b, u, place], dkv_ref.at[b, 0, :, columns(part, u)], g_recv.at[0]
        ).start()

    def send_attended(b, u):
        def a_step(k, _):
            i = u * GROUP + (k + me) % GROUP

            @pl.when(owner(i) != me)
            def _():
                a_copy(b, i).start()

            @pl.when(owner(i) == me)
            def _():
                pltpu.make_async_copy(abuf.at[b, i], att_ref.at[b, sample], a_recv.at[0]).start()
            return 0

        lax.fori_loop(0, GROUP, a_step, 0)

    def rep_copy(k):
        return pltpu.make_async_remote_copy(
            red_src.at[0], red_rep.at[rep], rep_send.at[k], sum_recv.at[0], device_id=rep_id(k)
        )

    def plane_copy(k):
        return pltpu.make_async_remote_copy(
            red_src.at[1], red_plane.at[me], plane_send.at[k], sum_recv.at[1], device_id={"mp": (me + k) % n_mp}
        )

    def rep_step(k, _):
        @pl.when(k != rep)
        def _():
            rep_copy(k).start()
        return 0

    def send_sums(gain_sum, gate_sum):
        red_src[0, 0:1] = gain_sum
        red_src[0, 1:2] = gate_sum
        lax.fori_loop(0, n_rep, rep_step, 0)
        pltpu.make_async_copy(red_src.at[0], red_rep.at[rep], sum_recv.at[0]).start()

    def unit(step, carry):
        gain_sum, gate_sum = carry
        b = step // OWN_KV
        u = step % OWN_KV
        heads = pl.ds(u * GROUP, GROUP)
        q_view, c_view = qbuf.at[b, heads], cbuf.at[b, heads]
        counts = count_v[b, pl.ds(sample, 1), :].astype(jnp.float32).astype(jnp.bfloat16)
        count_col = dot(spread, jnp.broadcast_to(counts, (HEAD, TEXT)), ((1,), (1,)))
        count_row = dot(jnp.broadcast_to(counts, (8, TEXT)), spread, ((1,), (1,)))[0:1]
        live = (count_col > 0.5).astype(jnp.float32)
        gate_live = gate * live
        limit = (jnp.maximum(count_row, 1.0) * PATCH).astype(jnp.int32)

        pltpu.make_async_copy(kvbuf.at[b, u], kvbuf.at[b, u], kv_recv.at[b, u]).wait()
        kv = kvbuf[b, u].reshape(KEYS, WIDE)
        raw = kv[:, :HEAD].astype(jnp.float32)
        values = kv[:, HEAD:]
        inverse = lax.rsqrt(jnp.mean(raw * raw, axis=-1, keepdims=True) + 1e-05)
        unit_key = raw * inverse
        keys = (unit_key * gain).astype(jnp.bfloat16)

        pltpu.make_async_copy(q_view, q_view, q_recv.at[b, u]).wait()
        queries = q_view[...].reshape(ROWS, HEAD)
        logits = dot(keys, queries, ((1,), (1,))) * SCALE
        logits = jnp.where(key_row < limit, logits, -1e30)
        exps = jnp.exp(logits - jnp.max(logits, axis=0, keepdims=True))
        probs = exps / jnp.sum(exps, axis=0, keepdims=True)
        probs_low = probs.astype(jnp.bfloat16)
        mixed = dot(probs_low, values, ((0,), (0,)))
        abuf[b, heads] = (gate_live * mixed).astype(jnp.bfloat16).reshape(GROUP, TEXT, HEAD)

        @pl.when(step < MICRO * OWN_KV - HOLD_A)
        def _():
            send_attended(b, u)

        pltpu.make_async_copy(c_view, c_view, c_recv.at[b, u]).wait()
        cotan = c_view[...].reshape(ROWS, HEAD).astype(jnp.float32)
        gate_sum = gate_sum + jnp.sum(cotan * live * mixed, axis=0, keepdims=True)
        d_mixed = (gate_live * cotan).astype(jnp.bfloat16)
        d_probs = dot(values, d_mixed, ((1,), (1,)))
        inner = jnp.sum(probs * d_probs, axis=0, keepdims=True)
        d_logits = (probs * (d_probs - inner) * SCALE).astype(jnp.bfloat16)
        for h in range(GROUP):
            rows, cols = slice(h * TEXT, (h + 1) * TEXT), slice(h * HEAD, (h + 1) * HEAD)
            qblk[rows, cols] = queries[rows]
            dblk[rows, cols] = d_mixed[rows]

        def head_sum(left, blocks):
            total = jnp.zeros((KEYS, HEAD), jnp.float32)
            for h in range(0, GROUP, 2):
                pair = dot(left, blocks[:, h * HEAD:(h + 2) * HEAD], ((1,), (0,)))
                pair = pair.astype(jnp.bfloat16).astype(jnp.float32)
                total = total + pair[:, :HEAD] + pair[:, HEAD:]
            return total.astype(jnp.bfloat16)

        key_part = head_sum(d_logits, qblk).astype(jnp.float32)
        gain_sum = gain_sum + jnp.sum(key_part * unit_key, axis=0, keepdims=True)

        @pl.when(step == MICRO * OWN_KV - 1)
        def _():
            send_sums(gain_sum, gate_sum)

        value_part = head_sum(probs_low, dblk)
        scaled = key_part * gain
        d_key = inverse * (scaled - unit_key * jnp.mean(scaled * unit_key, axis=-1, keepdims=True))
        gbuf[b, u, :, :, :HEAD] = d_key.astype(jnp.bfloat16).reshape(TILES, PATCH, HEAD)
        gbuf[b, u, :, :, HEAD:] = value_part.reshape(TILES, PATCH, HEAD)


        @pl.when(step < jnp.where(first_half, GRADS_AT_ONCE[0], GRADS_AT_ONCE[1]))
        def _():
            send_grads(b, u)

        return gain_sum, gate_sum

    zero = jnp.zeros((1, HEAD), jnp.float32)
    lax.fori_loop(0, MICRO * OWN_KV, unit, (zero, zero))

    def after_sums(i):
        for half, when in ((0, first_half), (1, jnp.logical_not(first_half))):
            @pl.when(when)
            def _():
                for step in GRADS_AFTER[half][i]:
                    send_grads(step // OWN_KV, step % OWN_KV)

    def plane_step(k, _):
        plane_copy(k).start()
        return 0

    for step in range(MICRO * OWN_KV - HOLD_A, MICRO * OWN_KV):
        send_attended(step // OWN_KV, step % OWN_KV)
    after_sums(0)
    pltpu.make_async_copy(red_rep, red_rep, sum_recv.at[0]).wait()
    red_src[1] = jnp.sum(red_rep[...], axis=0)
    pltpu.make_async_copy(red_src.at[1], red_plane.at[me], sum_recv.at[1]).start()
    lax.fori_loop(1, n_mp, plane_step, 0)
    after_sums(1)

    def heads_sent(n, _):
        @pl.when(worker(n) != me)
        def _():
            for b in range(MICRO):
                q_copy(b, n).wait_send()
                c_copy(b, n).wait_send()

        @pl.when(owner(n) != me)
        def _():
            for b in range(MICRO):
                a_copy(b, n).wait_send()
        return 0

    def members_sent(i, _):
        @pl.when(i != place)
        def _():
            for b in range(MICRO):
                for u in range(OWN_KV):
                    kv_copy(b, u, i).wait_send()
                    g_copy(b, u, i).wait_send()
        return 0

    def reps_sent(k, _):
        @pl.when(k != rep)
        def _():
            rep_copy(k).wait_send()
        return 0

    def plane_sent(k, _):
        plane_copy(k).wait_send()
        return 0

    lax.fori_loop(0, SAMPLES, heads_sent, 0)
    lax.fori_loop(0, TILES, members_sent, 0)
    lax.fori_loop(0, n_rep, reps_sent, 0)
    lax.fori_loop(1, n_mp, plane_sent, 0)

    pltpu.make_async_copy(red_plane, red_plane, sum_recv.at[1]).wait()
    total = jnp.sum(red_plane[...], axis=0)
    dgain_ref[...] = total[0:1]
    dgate_ref[...] = jnp.broadcast_to(jnp.sum(total[1:2], axis=1, keepdims=True) * (1.0 - gate * gate), (1, HEAD))

    pltpu.make_async_copy(att_ref, att_ref, a_recv.at[0]).wait()
    pltpu.make_async_copy(dkv_ref, dkv_ref, g_recv.at[0]).wait()


def shards(key_value, key_gain, queries, tile_count, attn_gate, cotangent):
    n_rep = lax.axis_size("dp") * lax.axis_size("segment")
    n_mp = lax.axis_size("mp")
    vmem, anywhere = pl.BlockSpec(memory_space=pltpu.VMEM), pl.BlockSpec(memory_space=pl.ANY)
    hbm = pl.BlockSpec(memory_space=pltpu.HBM)
    dma = pltpu.SemaphoreType.DMA
    bf16, f32 = jnp.bfloat16, jnp.float32
    gain_row = key_gain.reshape(1, HEAD)
    key_value, gain_row, queries, tile_count, cotangent = (
        pltpu.with_memory_space_constraint(x, pltpu.HBM)
        for x in (key_value, gain_row, queries, tile_count, cotangent)
    )
    attended, d_key_value, d_gain, d_gate = pl.pallas_call(
        kernel,
        out_shape=(
            jax.ShapeDtypeStruct(queries.shape, bf16),
            jax.ShapeDtypeStruct(key_value.shape, bf16),
            jax.ShapeDtypeStruct((1, HEAD), f32),
            jax.ShapeDtypeStruct((1, HEAD), f32),
        ),
        in_specs=[hbm, hbm, hbm, hbm, pl.BlockSpec(memory_space=pltpu.SMEM), hbm],
        out_specs=(anywhere, anywhere, vmem, vmem),
        scratch_shapes=[
            pltpu.VMEM((MICRO, OWN_KV, TILES, PATCH, WIDE), bf16),
            pltpu.VMEM((MICRO, OWN_HEADS, TEXT, HEAD), bf16),
            pltpu.VMEM((MICRO, OWN_HEADS, TEXT, HEAD), bf16),
            pltpu.VMEM((MICRO, OWN_KV, TILES, PATCH, WIDE), bf16),
            pltpu.VMEM((MICRO, OWN_HEADS, TEXT, HEAD), bf16),
            pltpu.VMEM((ROWS, GROUP * HEAD), bf16),
            pltpu.VMEM((ROWS, GROUP * HEAD), bf16),
            pltpu.VMEM((2, 2, HEAD), f32),
            pltpu.VMEM((n_rep, 2, HEAD), f32),
            pltpu.VMEM((n_mp, 2, HEAD), f32),
            dma((MICRO, OWN_KV, TILES)), dma((MICRO, OWN_KV)),
            dma((MICRO, SAMPLES)), dma((MICRO, OWN_KV)),
            dma((MICRO, SAMPLES)), dma((MICRO, OWN_KV)),
            dma((MICRO, OWN_KV, TILES)), dma((1,)),
            dma((MICRO, OWN_HEADS)), dma((1,)),
            dma((n_rep,)), dma((n_mp,)), dma((2,)),
            pltpu.VMEM((1, HEAD), f32), pltpu.VMEM(tile_count.shape, jnp.int32), dma((2,)),
            pltpu.SemaphoreType.REGULAR, pltpu.SemaphoreType.REGULAR, pltpu.SemaphoreType.REGULAR,
        ],
        compiler_params=pltpu.CompilerParams(
            collective_id=0, has_side_effects=True, vmem_limit_bytes=48 * 1024 * 1024
        ),
        name="cross_attention",
    )(key_value, gain_row, queries, tile_count, attn_gate, cotangent)
    return attended, d_key_value, d_gain.reshape(HEAD), d_gate[0, :1]


def solution(mesh):
    in_specs = (
        P("dp", ("segment", "mp"), None, None),
        P(),
        P("dp", "segment", None, "mp"),
        P("dp", "segment", None),
        P(),
        P("dp", "segment", None, "mp"),
    )
    out_specs = (P("dp", "segment", None, "mp"), P("dp", ("segment", "mp"), None, None), P(), P())
    return jax.shard_map(shards, mesh=mesh, in_specs=in_specs, out_specs=out_specs, check_vma=False)
```
